128 devices in a mesh: dp: 16 (over y, x), mp: 8 (over z, core).
Axes of the slice: x: 4, y: 4, z: 4, core: 2. Of those that a mesh axis runs over, the one named last changes fastest.
Arguments:
- hidden_in: bfloat16 [16384, 1024], P(('dp', 'mp')), may hold values from -6 to 6
- cotangent: float32 [16384, 1024], P(('dp', 'mp')), may hold values from -6 to 6
- segments: int32 [16384], P('dp'), may hold values from 0 to 47, as said below
- qkv_weight: bfloat16 [2, 1024, 3072], P(None, None, 'mp'), may hold values from -0.1875 to 0.1875
- out_weight: bfloat16 [2, 1024, 1024], P(None, 'mp'), may hold values from -3 to 3
- up_weight: bfloat16 [2, 1024, 4096], P(None, None, 'mp'), may hold values from -0.1875 to 0.1875
- down_weight: bfloat16 [2, 4096, 1024], P(None, 'mp'), may hold values from -0.09375 to 0.09375
- query_down: float32 [2, 1024, 128], replicated, may hold values from -0.1875 to 0.1875
- query_up: float32 [2, 128, 3072], replicated, may hold values from -0.5 to 0.5
- output_down: float32 [2, 1024, 128], replicated, may hold values from -3 to 3
- output_up: float32 [2, 128, 1024], replicated, may hold values from -0.5 to 0.5
- expand_down: float32 [2, 1024, 128], replicated, may hold values from -0.1875 to 0.1875
- expand_up: float32 [2, 128, 4096], replicated, may hold values from -0.5 to 0.5
- shrink_down: float32 [2, 4096, 128], replicated, may hold values from -0.09375 to 0.09375
- shrink_up: float32 [2, 128, 1024], replicated, may hold values from -0.5 to 0.5
- norm_params: float32 [2, 4, 1024], replicated, may hold values from -0.6 to 1.3
- norm_first: float32 [2, 4, 1024], replicated, may hold values from -40 to 40
- norm_second: float32 [2, 4, 1024], replicated, may hold values from 3440.64 to 221185
- owner_slot: int32 [256], replicated, may hold values from 0 to 383, as said below
- left_stats: float32 [384, 128, 128], P(('dp', 'mp')), may hold values from -1.3123902 to 56.832
- right_stats: float32 [384, 128, 128], P(('dp', 'mp')), may hold values from -1.3123902 to 56.832
- left_roots: float32 [384, 128, 128], P(('dp', 'mp')), may hold values from -0.007638725 to 0.3323935
- right_roots: float32 [384, 128, 128], P(('dp', 'mp')), may hold values from -0.007638725 to 0.3323935
Outputs:
- hidden_out: float32 [16384, 1024], P(('dp', 'mp'))
- hidden_grad: float32 [16384, 1024], P(('dp', 'mp'))
- adapter_grad: float32 [384, 128, 128], P(('dp', 'mp'))
- new_left: float32 [384, 128, 128], P(('dp', 'mp'))
- new_right: float32 [384, 128, 128], P(('dp', 'mp'))
- new_query_down: float32 [2, 1024, 128], replicated
- new_query_up: float32 [2, 128, 3072], replicated
- new_output_down: float32 [2, 1024, 128], replicated
- new_output_up: float32 [2, 128, 1024], replicated
- new_expand_down: float32 [2, 1024, 128], replicated
- new_expand_up: float32 [2, 128, 4096], replicated
- new_shrink_down: float32 [2, 4096, 128], replicated
- new_shrink_up: float32 [2, 128, 1024], replicated
- norm_moment: float32 [2, 4, 1024], replicated
- norm_square: float32 [2, 2, 1024], replicated
- expand_square: float32 [2, 2, 1024], replicated
- norm_new: float32 [2, 4, 1024], replicated
The draws below stay inside these ranges and needn't reach their ends.
Inputs may be any that keep to these rules, and one draw needn't show every extreme that they name: `segments`: numbers never fall along the tokens, and no two sequences of 1024 tokens share one. `owner_slot`: no slot is named twice.
All inputs are finite; a program needn't handle non-finite values.
Results may differ from the reference program's by a relative error of at most 0.029.
Values may be sent and summed in bfloat16 or wider, within the bound.
A program may use at most 320 MiB of HBM per device.

```python
import math
import jax
import jax.numpy as jnp
from jax import lax

D = 1024
HEADS = 16
HD = 64
FF = 4096
ROT = 16
ADAPTER_RANK = 128
LAYERS = 2
LEN = 1024
QBLK = 512
ADAM_STEP = 10
TOKENS = 16384
PIECE = 128
ADAPTER_BLOCKS = 256
STAT_SLOTS = 384


def symmetric_draw(key, frozen_output, spread_rows):
    diagonal_seed, remaining_seed = jax.random.split(key)
    diagonal_mask = frozen_output * jnp.exp(jax.random.uniform(diagonal_seed, (STAT_SLOTS, ADAPTER_RANK), jnp.float32, 0.0, math.log(4.0)))
    upper_mask = jnp.triu(jax.random.uniform(remaining_seed, (STAT_SLOTS, ADAPTER_RANK, ADAPTER_RANK), jnp.float32, -spread_rows, spread_rows), 1)
    return upper_mask + jnp.swapaxes(upper_mask, 1, 2) + diagonal_mask[:, :, None] * jnp.eye(ADAPTER_RANK, dtype=jnp.float32)[None]


def draw_segments(key, part):
    key = jax.random.fold_in(key, 11)
    opening_key, closing_key = jax.random.split(key)
    row_count = TOKENS // LEN
    opening = jax.random.randint(opening_key, (row_count, 1), 1, PIECE)
    closing = jax.random.randint(closing_key, (row_count, 1), 1, PIECE)
    position = jnp.arange(LEN, dtype=jnp.int32)[None, :]
    within = (position >= opening).astype(jnp.int32) + (position >= LEN - closing).astype(jnp.int32)
    return (within + 3 * jnp.arange(row_count, dtype=jnp.int32)[:, None]).reshape(TOKENS).astype(jnp.int32)


def draw_owner_slot(key, part):
    key = jax.random.fold_in(key, 23)
    dropout_seed, order_key = jax.random.split(key)
    inner_hidden = 1 + jax.random.permutation(dropout_seed, STAT_SLOTS - 2)
    dropout_rows = inner_hidden[:STAT_SLOTS - ADAPTER_BLOCKS]
    slot_flags = jnp.zeros((STAT_SLOTS,), jnp.int32).at[dropout_rows].set(1)
    retained_slots = jnp.argsort(slot_flags * STAT_SLOTS + jnp.arange(STAT_SLOTS, dtype=jnp.int32), stable=True)[:ADAPTER_BLOCKS]
    return retained_slots[jax.random.permutation(order_key, ADAPTER_BLOCKS)].astype(jnp.int32)


def draw_norm_params(key, part):
    key = jax.random.fold_in(key, 5)
    gain_key, shift_key = jax.random.split(key)
    gains = 1.0 + jax.random.uniform(gain_key, (LAYERS, 2, D), jnp.float32, -0.3, 0.3)
    shifts = jax.random.uniform(shift_key, (LAYERS, 2, D), jnp.float32, -0.6, 0.6)
    return jnp.stack([gains[:, 0], shifts[:, 0], gains[:, 1], shifts[:, 1]], axis=1)


def draw_norm_second(key, part):
    key = jax.random.fold_in(key, 53)
    attend_base = 3.4 * TOKENS * D / LEN
    expand_base = 0.21 * TOKENS
    base_rows = jnp.array([attend_base, attend_base, expand_base, expand_base], jnp.float32)[None, :, None]
    factor = jnp.exp(jax.random.uniform(key, (LAYERS, 4, D), jnp.float32, 0.0, math.log(3.95)))
    return base_rows * factor


def draw_left_stats(key, part):
    key = jax.random.fold_in(key, 31)
    frozen_output = 0.111 * ADAPTER_RANK
    return symmetric_draw(key, frozen_output, 1.04 * frozen_output * ADAPTER_RANK ** (-0.5))


def draw_right_stats(key, part):
    key = jax.random.fold_in(key, 37)
    frozen_output = 0.111 * ADAPTER_RANK
    return symmetric_draw(key, frozen_output, 1.04 * frozen_output * ADAPTER_RANK ** (-0.5))


def draw_left_roots(key, part):
    key = jax.random.fold_in(key, 41)
    frozen_output = (0.01 * ADAPTER_RANK * TOKENS) ** (-0.25)
    return symmetric_draw(key, frozen_output, 1.04 * frozen_output * ADAPTER_RANK ** (-0.5))


def draw_right_roots(key, part):
    key = jax.random.fold_in(key, 43)
    frozen_output = (0.01 * ADAPTER_RANK * TOKENS) ** (-0.25)
    return symmetric_draw(key, frozen_output, 1.04 * frozen_output * ADAPTER_RANK ** (-0.5))


def level_of(rng, shape, cuts, low, high):
    gain = 1.0
    for axis_at, blocks in cuts:
        steps = jax.random.uniform(jax.random.fold_in(jax.random.fold_in(rng, 6), axis_at), (blocks,), jnp.float32, low / len(cuts), high / len(cuts))
        gain = gain * jnp.repeat(jnp.exp(steps), shape[axis_at] // blocks).reshape((-1,) + (1,) * (len(shape) - 1 - axis_at))
    return gain


def noise(stream_key, dims, scale, reach, shards=(), kind=jnp.bfloat16):
    drawn = scale * jax.random.normal(stream_key, dims, jnp.float32)
    if shards:
        drawn = drawn * level_of(stream_key, dims, shards, -0.22, 0.18)
    return jnp.clip(drawn, -reach, reach).astype(kind)


def setup_inputs(seed: int = 0) -> dict:
    streams_of = jax.random.split(jax.random.key(seed), 24)
    hidden_in = noise(streams_of[0], (TOKENS, D), 1.0, 6.0, ((0, 128),))
    cotangent = noise(streams_of[1], (TOKENS, D), 1.0, 6.0, ((0, 128),), jnp.float32)
    segments = draw_segments(jax.random.fold_in(streams_of[23], 71), 0)
    qkv_weight = noise(streams_of[3], (LAYERS, D, 3 * D), D ** -0.5, 0.1875, ((2, 8),))
    out_weight = noise(streams_of[4], (LAYERS, D, D), 4 ** -0.5, 3.0, ((1, 8),))
    up_weight = noise(streams_of[5], (LAYERS, D, FF), D ** -0.5, 0.1875, ((2, 8),))
    down_weight = noise(streams_of[6], (LAYERS, FF, D), FF ** -0.5, 0.09375, ((1, 8),))
    query_down = noise(streams_of[7], (LAYERS, D, ADAPTER_RANK), D ** -0.5, 0.1875, (), jnp.float32)
    query_up = noise(streams_of[8], (LAYERS, ADAPTER_RANK, 3 * D), ADAPTER_RANK ** -0.5, 0.5, (), jnp.float32)
    output_down = noise(streams_of[9], (LAYERS, D, ADAPTER_RANK), 4 ** -0.5, 3.0, (), jnp.float32)
    output_up = noise(streams_of[10], (LAYERS, ADAPTER_RANK, D), ADAPTER_RANK ** -0.5, 0.5, (), jnp.float32)
    expand_down = noise(streams_of[11], (LAYERS, D, ADAPTER_RANK), D ** -0.5, 0.1875, (), jnp.float32)
    expand_up = noise(streams_of[12], (LAYERS, ADAPTER_RANK, FF), ADAPTER_RANK ** -0.5, 0.5, (), jnp.float32)
    shrink_down = noise(streams_of[13], (LAYERS, FF, ADAPTER_RANK), FF ** -0.5, 0.09375, (), jnp.float32)
    shrink_up = noise(streams_of[14], (LAYERS, ADAPTER_RANK, D), ADAPTER_RANK ** -0.5, 0.5, (), jnp.float32)
    norm_params = draw_norm_params(jax.random.fold_in(streams_of[23], 71), 0)
    norm_first = noise(streams_of[16], (LAYERS, 4, D), (0.055 * TOKENS ** 0.5), 40.0, (), jnp.float32)
    norm_second = draw_norm_second(jax.random.fold_in(streams_of[23], 71), 0)
    owner_slot = draw_owner_slot(jax.random.fold_in(streams_of[23], 71), 0)
    left_stats = draw_left_stats(jax.random.fold_in(streams_of[23], 71), 0)
    right_stats = draw_right_stats(jax.random.fold_in(streams_of[23], 71), 0)
    left_roots = draw_left_roots(jax.random.fold_in(streams_of[23], 71), 0)
    right_roots = draw_right_roots(jax.random.fold_in(streams_of[23], 71), 0)
    return {"hidden_in": hidden_in, "cotangent": cotangent, "segments": segments, "qkv_weight": qkv_weight, "out_weight": out_weight, "up_weight": up_weight, "down_weight": down_weight, "query_down": query_down, "query_up": query_up, "output_down": output_down, "output_up": output_up, "expand_down": expand_down, "expand_up": expand_up, "shrink_down": shrink_down, "shrink_up": shrink_up, "norm_params": norm_params, "norm_first": norm_first, "norm_second": norm_second, "owner_slot": owner_slot, "left_stats": left_stats, "right_stats": right_stats, "left_roots": left_roots, "right_roots": right_roots}


PRECISE_SETTING = lax.Precision.HIGHEST
NORM_EPS = 1e-05
ADAPTER_FACTOR = 0.5
STAT_DECAY = 0.9
ADAPT_RATE = 0.4
STEP_EPS = 1e-06
MOMENT_DECAY = 0.9
SQUARE_DECAY = 0.95
NORM_RATE = 1.0
ADAM_EPS = 1e-08
MASKED = -1e+30

@jax.custom_vjp
def low(v):
    return lax.optimization_barrier(v.astype(jnp.bfloat16)).astype(jnp.float32)

@jax.custom_vjp
def lowrank_backward(v):
    return v

def low_keep(v):
    return (low(v), None)

def low_pass(kept, grad):
    return (grad,)

def back_keep(v):
    return (v, None)

def back_low(kept, grad):
    return (low(grad),)
low.defvjp(low_keep, low_pass)
lowrank_backward.defvjp(back_keep, back_low)

def precise_product(former, latter):
    return jnp.dot(former, latter, precision=PRECISE_SETTING, preferred_element_type=jnp.float32)

def normalize(values, gain_row, shift_row):
    average = lax.optimization_barrier(jnp.mean(values, axis=-1, keepdims=True))
    centred = values - average
    variance = lax.optimization_barrier(jnp.mean(centred * centred, axis=-1, keepdims=True))
    return centred * lax.rsqrt(variance + NORM_EPS) * gain_row + shift_row

def angles_of(segment_ids):
    position = jnp.arange(segment_ids.shape[0], dtype=jnp.int32)
    starts = jnp.concatenate([jnp.ones((1,), dtype=bool), segment_ids[1:] != segment_ids[:-1]])
    begins = lax.cummax(jnp.where(starts, position, 0), axis=0)
    offset = (position - begins).astype(jnp.float32)
    frequency = jnp.exp(jnp.arange(ROT // 2, dtype=jnp.float32) * (-2.0 * math.log(10000.0) / ROT))
    phases = offset[:, None] * frequency[None, :]
    phases = jnp.concatenate([phases, phases], axis=-1)
    return (jnp.cos(phases)[:, None, :], jnp.sin(phases)[:, None, :])

def rotate(values, cos_table, sin_table):
    halfway = ROT // 2
    leading = values[..., :ROT]
    turned = jnp.concatenate([-leading[..., halfway:], leading[..., :halfway]], axis=-1)
    return jnp.concatenate([leading * cos_table + turned * sin_table, values[..., ROT:]], axis=-1)

def split_blocks(matrix, by_columns):
    if by_columns:
        return matrix.reshape(ADAPTER_RANK, matrix.shape[1] // ADAPTER_RANK, ADAPTER_RANK).transpose(1, 0, 2)
    return matrix.reshape(matrix.shape[0] // ADAPTER_RANK, ADAPTER_RANK, ADAPTER_RANK)

def pack_blocks(adapters):
    pieces = []
    for layer_idx in range(adapters[0].shape[0]):
        for kind_idx, matrix in enumerate(adapters):
            pieces.append(split_blocks(matrix[layer_idx], kind_idx % 2 == 1))
    return jnp.concatenate(pieces, axis=0)

def unpack_blocks(blocks, templates):
    results = [[] for listed in templates]
    cursor = 0
    for layer_idx in range(templates[0].shape[0]):
        for kind_idx, matrix in enumerate(templates):
            dims_of = matrix.shape[1:]
            amount = dims_of[0] // ADAPTER_RANK * (dims_of[1] // ADAPTER_RANK)
            portion = blocks[cursor:cursor + amount]
            if kind_idx % 2 == 1:
                portion = portion.transpose(1, 0, 2).reshape(dims_of)
            else:
                portion = portion.reshape(dims_of)
            results[kind_idx].append(portion)
            cursor += amount
    return tuple((jnp.stack(listed) for listed in results))

def precondition(gradients, weights, left_old, right_old, left_root, right_root):
    grad_scale = 1.0 / (lax.optimization_barrier(jnp.mean(gradients * gradients, axis=(1, 2), keepdims=True)) + STEP_EPS)
    left_new = STAT_DECAY * left_old + (1 - STAT_DECAY) * jnp.einsum('sij,skj->sik', gradients, gradients, precision=PRECISE_SETTING) * grad_scale
    right_new = STAT_DECAY * right_old + (1 - STAT_DECAY) * jnp.einsum('sji,sjk->sik', gradients, gradients, precision=PRECISE_SETTING) * grad_scale
    direction = jnp.einsum('sij,sjk->sik', left_root, gradients, precision=PRECISE_SETTING)
    direction = jnp.einsum('sij,sjk->sik', direction, right_root, precision=PRECISE_SETTING)
    normalizer = lax.rsqrt(lax.optimization_barrier(jnp.mean(direction * direction, axis=(1, 2), keepdims=True)) + STEP_EPS)
    weight_scale = jnp.sqrt(lax.optimization_barrier(jnp.mean(weights * weights, axis=(1, 2), keepdims=True)) + STEP_EPS)
    return (left_new, right_new, weights - ADAPT_RATE * weight_scale * direction * normalizer)

def attention(queries, keys, values, segment_row):
    position = jnp.arange(LEN, dtype=jnp.int32)

    def one_block(block_idx):
        first_row = block_idx * QBLK
        query_blk = lax.dynamic_slice_in_dim(queries, first_row, QBLK, 0)
        seg_block = lax.dynamic_slice_in_dim(segment_row, first_row, QBLK, 0)
        pos_block = lax.dynamic_slice_in_dim(position, first_row, QBLK, 0)
        scores = lowrank_backward(jnp.einsum('qhe,khe->hqk', query_blk, keys, precision=PRECISE_SETTING))
        allowed = (seg_block[:, None] == segment_row[None, :]) & (pos_block[:, None] >= position[None, :])
        scores = jnp.where(allowed[None], scores, MASKED)
        highest = lax.optimization_barrier(jnp.max(scores, axis=-1, keepdims=True))
        weights = jnp.exp(scores - highest)
        weights_low = low(weights / lax.optimization_barrier(jnp.sum(weights, axis=-1, keepdims=True)))
        return jnp.einsum('hqk,khe->qhe', weights_low, values, precision=PRECISE_SETTING)
    blocks = lax.map(jax.checkpoint(one_block), jnp.arange(LEN // QBLK, dtype=jnp.int32))
    return blocks.reshape(LEN, HEADS * HD)

def layer_forward(stream, segment_row, tables, frozen, adapted_rows, norm_set):
    query_key_value_matrix, output_matrix, up_matrix, down_matrix = frozen
    query_in, query_output, attend_in, attention_output, expand_in, expansion_output, shrink_in, contract_output = [low(matrix) for matrix in adapted_rows]
    cos_table, sin_table = tables
    first_rows = low(normalize(stream, norm_set[0], norm_set[1]))
    second_rows = low(normalize(stream, norm_set[2], norm_set[3]))
    lowrank_query = low(precise_product(first_rows, query_in))
    mixture_rows = lowrank_backward(precise_product(first_rows, query_key_value_matrix) + ADAPTER_FACTOR * precise_product(lowrank_query, query_output))
    mixture_rows = mixture_rows.reshape(LEN, HEADS, 3, HD)
    query_heads = low(rotate(mixture_rows[:, :, 0], cos_table, sin_table) * HD ** (-0.5))
    key_heads = low(rotate(mixture_rows[:, :, 1], cos_table, sin_table))
    value_heads = low(mixture_rows[:, :, 2])
    attention_rows = low(lowrank_backward(attention(query_heads, key_heads, value_heads, segment_row)))
    inner_attention = lowrank_backward(precise_product(attention_rows, attend_in))
    lowrank_expansion = low(precise_product(second_rows, expand_in))
    preactivation = lowrank_backward(precise_product(second_rows, up_matrix) + ADAPTER_FACTOR * precise_product(lowrank_expansion, expansion_output))
    active_flags = low(jax.nn.gelu(preactivation, approximate=False))
    inner_contract = lowrank_backward(precise_product(active_flags, shrink_in))
    adapter_branch = precise_product(attention_rows, output_matrix) + precise_product(active_flags, down_matrix) + ADAPTER_FACTOR * (precise_product(inner_attention, attention_output) + precise_product(inner_contract, contract_output))
    return stream + lowrank_backward(adapter_branch)

def stack_forward(stream, segment_row, frozen, adapters, norm_params):
    tables = angles_of(segment_row)
    for layer_idx in range(LAYERS):
        stream = layer_forward(stream, segment_row, tables, [weight[layer_idx] for weight in frozen], [matrix[layer_idx] for matrix in adapters], norm_params[layer_idx])
    return stream

def reference(hidden_in, cotangent, segments, qkv_weight, out_weight, up_weight, down_weight, query_down, query_up, output_down, output_up, expand_down, expand_up, shrink_down, shrink_up, norm_params, norm_first, norm_second, owner_slot, left_stats, right_stats, left_roots, right_roots):
    frozen = tuple((weight.astype(jnp.float32) for weight in (qkv_weight, out_weight, up_weight, down_weight)))
    adapters = (query_down, query_up, output_down, output_up, expand_down, expand_up, shrink_down, shrink_up)
    row_count = TOKENS // LEN
    inputs = hidden_in.astype(jnp.float32).reshape(row_count, LEN, D)
    tangents = cotangent.reshape(row_count, LEN, D)
    seg_rows = segments.reshape(row_count, LEN)

    def one_row(running, packed):
        stream_row, tangent_row, segment_row = packed

        def forward(stream, adapt_set, norm_set):
            return stack_forward(stream, segment_row, frozen, adapt_set, norm_set)
        output, pullback = jax.vjp(forward, stream_row, adapters, norm_params)
        grad_stream, grad_adapt, grad_norm = pullback(tangent_row)
        running = jax.tree.map(lambda former, latter: former + latter, running, (grad_adapt, grad_norm))
        return (running, (output, grad_stream))
    initial = jax.tree.map(jnp.zeros_like, (adapters, norm_params))
    (grad_adapt, grad_norm), (outputs, grad_inputs) = lax.scan(one_row, initial, (inputs, tangents, seg_rows))
    slot_total = left_stats.shape[0]

    def slots_of(blocks):
        return jnp.zeros((slot_total, ADAPTER_RANK, ADAPTER_RANK), jnp.float32).at[owner_slot].set(blocks)
    grad_slots = slots_of(pack_blocks(grad_adapt))
    left_new, right_new, stepped = precondition(grad_slots, slots_of(pack_blocks(adapters)), left_stats, right_stats, left_roots, right_roots)
    renewed = unpack_blocks(stepped[owner_slot], adapters)
    moment = MOMENT_DECAY * norm_first + (1 - MOMENT_DECAY) * grad_norm
    square = SQUARE_DECAY * norm_second + (1 - SQUARE_DECAY) * grad_norm * grad_norm
    renewed_norms = norm_params - NORM_RATE * (moment / (1 - MOMENT_DECAY ** ADAM_STEP)) / (jnp.sqrt(square / (1 - SQUARE_DECAY ** ADAM_STEP)) + ADAM_EPS)
    return (outputs.reshape(TOKENS, D), grad_inputs.reshape(TOKENS, D), grad_slots, left_new, right_new, renewed[0], renewed[1], renewed[2], renewed[3], renewed[4], renewed[5], renewed[6], renewed[7], moment, square[:, :2], square[:, 2:], renewed_norms)
```

```python
from functools import partial
import math

import jax
import jax.numpy as jnp
import numpy as np
from jax import lax
from jax.experimental import pallas as pl
from jax.experimental.pallas import tpu as pltpu
from jax.sharding import PartitionSpec as P

D = 1024
HD = 64
FF = 4096
ROT = 16
RANK = 128
LAYERS = 2
LEN = 1024
PIECE = 128
PAIR = 256
HALF = 64
ADAM_STEP = 10
NORM_EPS = 1e-05
STAT_DECAY = 0.9
ADAPT_RATE = 0.4
STEP_EPS = 1e-06
MOMENT_DECAY = 0.9
SQUARE_DECAY = 0.95
NORM_RATE = 1.0
ADAM_EPS = 1e-08
MASKED = -1e30

MESH = pl.DeviceIdType.MESH
f32 = jnp.float32
bf16 = jnp.bfloat16
VMEM_LIMIT = 56 * 2**20


def nn(a, b):
    return lax.dot_general(a, b, (((1,), (0,)), ((), ())), preferred_element_type=f32)


def nt(a, b):
    return lax.dot_general(a, b, (((1,), (1,)), ((), ())), preferred_element_type=f32)


def tn(a, b):
    return lax.dot_general(a, b, (((0,), (0,)), ((), ())), preferred_element_type=f32)


def prep_kernel(member, qkv, qd, qu, od, ou, ed, eu, sd, su, wq_o, qu_o, od_o, oush_o, ed_o, eu_o, sd_o):
    def regroup(groups):
        low = lax.broadcasted_iota(jnp.int32, groups[0].shape, 1) < HD
        return (
            jnp.where(low, groups[0], groups[1]),
            pltpu.roll(jnp.where(low, groups[2], groups[0]), HD, 1),
            jnp.where(low, groups[1], groups[2]),
        )

    for i, part in enumerate(regroup([qkv[:, i * 128 : i * 128 + 128].astype(f32) for i in range(3)])):
        wq_o[:, i * 128 : i * 128 + 128] = part.astype(bf16)
    wq_o[:, 384:512] = qd[...].astype(bf16)
    for i, part in enumerate(regroup([qu[:, i * 128 : i * 128 + 128] for i in range(3)])):
        qu_o[:, i * 128 : i * 128 + 128] = (0.5 * part).astype(bf16)
    od_o[...] = od[...].astype(bf16)
    oush_o[0:128, :] = (0.5 * ou[...]).astype(bf16)
    oush_o[128:256, :] = (0.5 * su[...]).astype(bf16)
    ed_o[...] = ed[...].astype(bf16)
    eu_o[...] = (0.5 * eu[...]).astype(bf16)
    sd_o[...] = sd[...].astype(bf16)


def prepare(member, qkv, qd, qu, od, ou, ed, eu, sd, su):
    def whole(rows, cols):
        return pl.BlockSpec((None, rows, cols), lambda l, m: (l, 0, 0))

    def by_cols(rows, cols):
        return pl.BlockSpec((None, rows, cols), lambda l, m: (l, 0, m[0]))

    def by_rows(rows, cols):
        return pl.BlockSpec((None, rows, cols), lambda l, m: (l, m[0], 0))

    shapes = [(1024, 512), (128, 384), (128, 128), (256, 1024), (1024, 128), (128, 512), (512, 128)]
    return pl.pallas_call(
        prep_kernel,
        grid_spec=pltpu.PrefetchScalarGridSpec(
            num_scalar_prefetch=1,
            grid=(LAYERS,),
            in_specs=[
                whole(1024, 384),
                whole(1024, 128),
                by_cols(128, 384),
                by_rows(128, 128),
                whole(128, 1024),
                whole(1024, 128),
                by_cols(128, 512),
                by_rows(512, 128),
                whole(128, 1024),
            ],
            out_specs=[whole(*s) for s in shapes],
        ),
        out_shape=[jax.ShapeDtypeStruct((LAYERS,) + s, bf16) for s in shapes],
        compiler_params=pltpu.CompilerParams(vmem_limit_bytes=VMEM_LIMIT),
        name="prep",
    )(member, qkv, qd, qu, od, ou, ed, eu, sd, su)


class Ring:
    def __init__(self):
        me = lax.axis_index("mp")
        z, c = me // 2, me % 2
        self.me, self.z, self.c = me, z, c
        self.zp, self.zm, self.z2 = (z + 1) % 4, (z + 3) % 4, (z + 2) % 4
        self.R, self.L, self.O = 2 * self.zp + c, 2 * self.zm + c, 2 * z + 1 - c

    def greet(self):
        barrier = pltpu.get_barrier_semaphore()
        for i in (self.R, self.L, self.O):
            pl.semaphore_signal(barrier, inc=1, device_id={"mp": i}, device_id_type=MESH)
        pl.semaphore_wait(barrier, 3)


def rcopy(src, dst, ssem, rsem, to):
    return pltpu.make_async_remote_copy(
        src_ref=src, dst_ref=dst, send_sem=ssem, recv_sem=rsem, device_id={"mp": to}, device_id_type=MESH
    )


def rows_at(start, size):
    return pl.ds(pl.multiple_of(start, size), size)


class Gather:
    def __init__(self, ring, full, ssem, rsem, piece=PIECE):
        self.ring, self.full, self.ssem, self.rsem = ring, full, ssem, rsem
        self.piece = piece

    def cp(self, idx, half, sem, to):
        if half is None:
            sl = rows_at(idx * self.piece, self.piece)
        else:
            sl = rows_at(idx * self.piece + half * (self.piece // 2), self.piece // 2)
        return rcopy(self.full.at[sl], self.full.at[sl], self.ssem.at[sem], self.rsem.at[sem], to)

    def start(self):
        r = self.ring
        self.cp(r.me, 0, 0, r.R).start()
        self.cp(r.me, 1, 1, r.L).start()
        self.cp(r.me, None, 6, r.O).start()
        self.cp(r.me, 1, 2, r.R).start()
        self.cp(r.me, 0, 3, r.L).start()

    def step(self, s):
        for n in range(4):
            pl.when(s == n)(partial(self.step_now, n))

    def step_now(self, n):
        r, cp = self.ring, self.cp
        O, R, L = r.O, r.R, r.L
        zl, zr, zq = 2 * r.zm + r.c, 2 * r.zp + r.c, 2 * r.z2 + r.c
        pl_, pr_, pq = 2 * r.zm + 1 - r.c, 2 * r.zp + 1 - r.c, 2 * r.z2 + 1 - r.c
        if n == 0:
            cp(O, None, 6, O).wait_recv()
        elif n == 1:
            cp(zl, 0, 0, R).wait_recv()
            cp(zl, 0, 4, R).start()
            cp(zl, 0, 7, O).start()
            cp(zr, 1, 1, L).wait_recv()
            cp(zr, 1, 5, L).start()
            cp(zr, 1, 8, O).start()
            cp(zl, 1, 2, R).wait_recv()
            cp(zl, 1, 9, O).start()
            cp(pl_, 0, 7, O).wait_recv()
            cp(pl_, 1, 9, O).wait_recv()
        elif n == 2:
            cp(zr, 0, 3, L).wait_recv()
            cp(zr, 0, 10, O).start()
            cp(pr_, 1, 8, O).wait_recv()
            cp(pr_, 0, 10, O).wait_recv()
        else:
            cp(zq, 0, 4, R).wait_recv()
            cp(zq, 0, 11, O).start()
            cp(zq, 1, 5, L).wait_recv()
            cp(zq, 1, 12, O).start()
            cp(pq, 0, 11, O).wait_recv()
            cp(pq, 1, 12, O).wait_recv()

    def pair(self, s):
        z = self.ring.z
        return (z + jnp.where(s == 0, 0, jnp.where(s == 1, 3, jnp.where(s == 2, 1, 2)))) % 4

    def finish(self):
        r = self.ring
        for sem in range(13):
            self.cp(r.me, None if sem == 6 else 0, sem, r.O).wait_send()


class Scatter:
    def __init__(self, ring, pb, prt, tr, fin, work, ssem, rsem):
        self.ring, self.pb, self.prt, self.tr, self.fin, self.work = ring, pb, prt, tr, fin, work
        self.ssem, self.rsem = ssem, rsem

    def pair(self, s):
        z = self.ring.z
        return (z + jnp.where(s == 0, 2, jnp.where(s == 1, 1, jnp.where(s == 2, 3, 0)))) % 4

    def cp(self, src, dst, sem, to):
        return rcopy(src, dst, self.ssem.at[sem], self.rsem.at[sem], to)

    def to_partner(self, s):
        r = self.ring
        theirs = self.pb.at[s, rows_at((1 - r.c) * PIECE, PIECE)]
        return self.cp(theirs, self.prt.at[s], s, r.O)

    def put(self, s, term):
        self.pb[s] = term.astype(bf16)
        self.to_partner(s).start()

    def summed(self, s):
        self.to_partner(s).wait_recv()
        own = self.pb[s, rows_at(self.ring.c * PIECE, PIECE)]
        return own.astype(f32) + self.prt[s].astype(f32)

    def h(self, i):
        return pl.ds(i * HALF, HALF)

    def c_tr0(self):
        return self.cp(self.work.at[0, self.h(0)], self.tr.at[0], 4, self.ring.R)

    def c_tr1(self):
        return self.cp(self.work.at[0, self.h(1)], self.tr.at[1], 5, self.ring.L)

    def c_r1(self):
        return self.cp(self.work.at[1, self.h(1)], self.fin.at[0, self.h(1)], 6, self.ring.R)

    def c_l0(self):
        return self.cp(self.work.at[2, self.h(0)], self.fin.at[1, self.h(0)], 7, self.ring.L)

    def c_r0(self):
        return self.cp(self.work.at[1, self.h(0)], self.fin.at[0, self.h(0)], 8, self.ring.R)

    def c_l1(self):
        return self.cp(self.work.at[2, self.h(1)], self.fin.at[1, self.h(1)], 9, self.ring.L)

    def step(self, s):
        @pl.when(s == 1)
        def _():
            self.work[0] = self.summed(0).astype(bf16)
            self.c_tr0().start()
            self.c_tr1().start()

        @pl.when(s == 2)
        def _():
            self.work[1] = self.summed(1).astype(bf16)
            self.c_r1().start()

        @pl.when(s == 3)
        def _():
            self.work[2] = self.summed(2).astype(bf16)
            self.c_l0().start()
            self.c_tr0().wait_recv()
            h0, h1 = self.h(0), self.h(1)
            self.work[1, h0] = (self.work[1, h0].astype(f32) + self.tr[0].astype(f32)).astype(bf16)
            self.c_r0().start()
            self.c_tr1().wait_recv()
            self.work[2, h1] = (self.work[2, h1].astype(f32) + self.tr[1].astype(f32)).astype(bf16)
            self.c_l1().start()

    def finish(self):
        total = self.summed(3)
        self.c_r1().wait_recv()
        self.c_l0().wait_recv()
        self.c_r0().wait_recv()
        self.c_l1().wait_recv()
        total = total + self.fin[0].astype(f32) + self.fin[1].astype(f32)
        for s in range(4):
            self.to_partner(s).wait_send()
        for c in (self.c_tr0, self.c_tr1, self.c_r1, self.c_l0, self.c_r0, self.c_l1):
            c().wait_send()
        return total


GATHER_SCRATCH = [pltpu.SemaphoreType.DMA((13,)), pltpu.SemaphoreType.DMA((13,))]
SCATTER_SCRATCH = [
    pltpu.VMEM((4, PAIR, D), bf16),
    pltpu.VMEM((4, PIECE, D), bf16),
    pltpu.VMEM((2, HALF, D), bf16),
    pltpu.VMEM((2, PIECE, D), bf16),
    pltpu.VMEM((3, PIECE, D), bf16),
    pltpu.SemaphoreType.DMA((10,)),
    pltpu.SemaphoreType.DMA((10,)),
]


def centred_rows(x):
    cen = x - jnp.mean(x, axis=-1, keepdims=True)
    rstd = lax.rsqrt(jnp.mean(cen * cen, axis=-1, keepdims=True) + NORM_EPS)
    return cen * rstd, rstd


def lane_in_head(shape):
    return lax.broadcasted_iota(jnp.int32, shape, 1) % HD


def rope(x, cos, sin):
    lane = lane_in_head(x.shape)
    turned = jnp.where(lane < ROT // 2, -pltpu.roll(x, 128 - ROT // 2, 1), pltpu.roll(x, ROT // 2, 1))
    return x * cos + turned * sin


def rope_back(g, cos, sin):
    lane = lane_in_head(g.shape)
    w = g * sin
    turned = jnp.where(
        lane < ROT // 2,
        pltpu.roll(w, 128 - ROT // 2, 1),
        jnp.where(lane < ROT, -pltpu.roll(w, ROT // 2, 1), 0.0),
    )
    return g * cos + turned


def allowed_keys(start_ref, k):
    keys = PAIR * (k + 1)
    kpos = lax.broadcasted_iota(jnp.int32, (keys, PAIR), 0)
    qpos = lax.broadcasted_iota(jnp.int32, (keys, PAIR), 1) + PAIR * k
    return (kpos >= start_ref[0:1, PAIR * k : PAIR * k + PAIR]) & (kpos <= qpos)


def forward_kernel(
    stream, norm, wq, qu, od, oush, ed, eu, sd, up, down, out_w, cos, sin, start,
    new_stream, x_o, q_o, k_o, v_o, att_o, act_o, gp_o, lq_o, le_o, ias_o, lse_o,
    xf, vt, ag_s, ag_r, pb, prt, tr, fin, work, rs_s, rs_r, osem,
):
    ring = Ring()
    gather = Gather(ring, xf, ag_s, ag_r)
    scatter = Scatter(ring, pb, prt, tr, fin, work, rs_s, rs_r)
    xhat, _ = centred_rows(stream[...])
    xf[rows_at(ring.me * PIECE, PIECE)] = xhat.astype(bf16)
    ring.greet()
    gather.start()

    def arrive(s, carry):
        gather.step(s)
        p = gather.pair(s)
        rows = rows_at(p * PAIR, PAIR)
        x = xf[rows].astype(f32)
        na = (x * norm[0:1, :] + norm[1:2, :]).astype(bf16)
        nb = (x * norm[2:3, :] + norm[3:4, :]).astype(bf16)
        m = nn(na, wq[...])
        lq = m[:, 384:512].astype(bf16)
        lq_o[rows] = lq
        m = m[:, 0:384] + nn(lq, qu[...])
        cs, sn = cos[rows], sin[rows]
        q_o[rows] = (rope(m[:, 0:128], cs, sn) * HD**-0.5).astype(bf16)
        k_o[rows] = rope(m[:, 128:256], cs, sn).astype(bf16)
        v = m[:, 256:384]
        v_o[rows] = v.astype(bf16)
        vt[:, rows] = v.T.astype(bf16)
        le = nn(nb, ed[...]).astype(bf16)
        le_o[rows] = le
        pre = nn(nb, up[...]) + nn(le, eu[...])
        cdf = 0.5 + 0.5 * lax.erf(pre * (0.5**0.5))
        act = (pre * cdf).astype(bf16)
        act_o[rows] = act
        gp_o[rows] = (cdf + pre * (jnp.exp(-0.5 * pre * pre) * ((2 * math.pi) ** -0.5))).astype(bf16)
        ias_o[rows, 128:256] = nn(act, sd[...]).astype(bf16)
        return carry

    lax.fori_loop(0, 4, arrive, 0)
    keep = pltpu.make_async_copy(xf, x_o, osem)
    keep.start()

    def attend(k):
        keys = PAIR * (k + 1)
        rows = slice(PAIR * k, PAIR * k + PAIR)
        ok = allowed_keys(start, k)
        qp = q_o[rows, :]
        head = lax.broadcasted_iota(jnp.int32, qp.shape, 1) // HD
        parts = []
        for h in range(2):
            qm = jnp.where(head == h, qp, jnp.zeros_like(qp))
            s = jnp.where(ok, nt(k_o[0:keys, :], qm), MASKED)
            top = jnp.max(s, axis=0, keepdims=True)
            e = jnp.exp(s - top)
            total = jnp.sum(e, axis=0, keepdims=True)
            lse_o[h : h + 1, rows] = top + jnp.log(total)
            o = nn(vt[h * HD : h * HD + HD, 0:keys], e.astype(bf16))
            parts.append(o / total)
        att_o[rows, :] = jnp.concatenate(parts, axis=0).T.astype(bf16)

    def leave(s, carry):
        p = scatter.pair(s)
        for k in range(4):
            pl.when(p == k)(partial(attend, k))
        rows = rows_at(p * PAIR, PAIR)
        att = att_o[rows]
        ias_o[rows, 0:128] = nn(att, od[...]).astype(bf16)
        term = nn(act_o[rows], down[...]) + nn(att, out_w[...]) + nn(ias_o[rows], oush[...])
        scatter.put(s, term)
        scatter.step(s)
        return carry

    lax.fori_loop(0, 4, leave, 0)
    new_stream[...] = stream[...] + scatter.finish()
    gather.finish()
    keep.wait()


def vmem_specs(n):
    return [pl.BlockSpec(memory_space=pltpu.VMEM)] * n


def layer_of(layer, rows, cols):
    return pl.BlockSpec((None, rows, cols), lambda i: (layer, 0, 0))


def plain(rows, cols):
    return pl.BlockSpec((rows, cols), lambda i: (0, 0))


def blocks(count, rows):
    return pl.BlockSpec((count, rows, 128), lambda i: (0, 0, 0))


WEIGHT_SHAPES = [(1024, 512), (128, 384), (128, 128), (256, 1024), (1024, 128), (128, 512), (512, 128),
                 (1024, 512), (512, 1024), (128, 1024)]


def forward_layer(layer, stream, norm_params, weights, tables):
    saved = [(LEN, 128), (LEN, 128), (LEN, 128), (LEN, 128), (LEN, 512), (LEN, 512), (LEN, 128), (LEN, 128), (LEN, 256)]
    return pl.pallas_call(
        forward_kernel,
        grid=(1,),
        in_specs=[plain(PIECE, D), layer_of(layer, 4, D)]
        + [layer_of(layer, *s) for s in WEIGHT_SHAPES]
        + [plain(LEN, 128), plain(LEN, 128), plain(1, LEN)],
        out_specs=[plain(PIECE, D), pl.BlockSpec(memory_space=pl.ANY)]
        + [plain(*s) for s in saved]
        + [plain(8, LEN)],
        out_shape=[jax.ShapeDtypeStruct((PIECE, D), f32), jax.ShapeDtypeStruct((LEN, D), bf16)]
        + [jax.ShapeDtypeStruct(s, bf16) for s in saved]
        + [jax.ShapeDtypeStruct((8, LEN), f32)],
        scratch_shapes=[pltpu.VMEM((LEN, D), bf16), pltpu.VMEM((128, LEN), bf16)]
        + GATHER_SCRATCH
        + SCATTER_SCRATCH
        + [pltpu.SemaphoreType.DMA],
        compiler_params=pltpu.CompilerParams(
            collective_id=layer, has_side_effects=True, vmem_limit_bytes=VMEM_LIMIT
        ),
        name="forward",
    )(stream, norm_params, *weights, *tables)


def backward_kernel(
    grad, stream, norm, wq, qu, od, oush, ed, eu, sd, up, down, out_w, cos, sin, start,
    xf, q, k, v, att, act, gp, lq, le, ias, lse,
    new_grad, own_g, all_g, norm_o,
    norm_g, db, dias, datt, dpre, dle, dxb, dq, dk, dv, dmix, kt, acc_q, acc_e, ag_s, ag_r, pb, prt, tr, fin, work, rs_s, rs_r,
):
    ring = Ring()
    gather = Gather(ring, db, ag_s, ag_r)
    scatter = Scatter(ring, pb, prt, tr, fin, work, rs_s, rs_r)
    db[rows_at(ring.me * PIECE, PIECE)] = grad[...].astype(bf16)
    ring.greet()
    gather.start()
    kt[...] = k[...].astype(f32).T.astype(bf16)
    norm_g[...] = jnp.zeros_like(norm_g)
    dk[...] = jnp.zeros_like(dk)
    dv[...] = jnp.zeros_like(dv)
    acc_q[...] = jnp.zeros_like(acc_q)
    acc_e[...] = jnp.zeros_like(acc_e)

    def arrive(s, carry):
        gather.step(s)
        p = gather.pair(s)
        rows = rows_at(p * PAIR, PAIR)
        d = db[rows]
        di = nt(d, oush[...]).astype(bf16)
        dias[rows] = di
        datt[rows] = (nt(d, out_w[...]) + nt(di[:, 0:128], od[...])).astype(bf16)
        dact = nt(d, down[...]) + nt(di[:, 128:256], sd[...])
        dp = (dact * gp[rows].astype(f32)).astype(bf16)
        dpre[rows] = dp
        dl = nt(dp, eu[...]).astype(bf16)
        dle[rows] = dl
        dnb = nt(dp, up[...]) + nt(dl, ed[...])
        x = xf[rows].astype(f32)
        norm_g[2:3, :] += jnp.sum(dnb * x, axis=0, keepdims=True)
        norm_g[3:4, :] += jnp.sum(dnb, axis=0, keepdims=True)
        dxb[rows] = dnb * norm[2:3, :]
        return carry

    lax.fori_loop(0, 4, arrive, 0)

    for blk in range(4):
        keys = PAIR * (blk + 1)
        rows = slice(PAIR * blk, PAIR * blk + PAIR)
        ok = allowed_keys(start, blk)
        qp, dp = q[rows, :], datt[rows, :]
        head = lax.broadcasted_iota(jnp.int32, qp.shape, 1) // HD
        parts = []
        for h in range(2):
            qm = jnp.where(head == h, qp, jnp.zeros_like(qp))
            dm = jnp.where(head == h, dp, jnp.zeros_like(dp))
            prob = jnp.where(ok, jnp.exp(nt(k[0:keys, :], qm) - lse[h : h + 1, rows]), 0.0)
            weighted = prob * nt(v[0:keys, :], dm)
            ds = (weighted - prob * jnp.sum(weighted, axis=0, keepdims=True)).astype(bf16)
            dv[0:keys, :] += nn(prob.astype(bf16), dm)
            dk[0:keys, :] += nn(ds, qm)
            parts.append(nn(kt[h * HD : h * HD + HD, 0:keys], ds))
        dq[rows, :] = jnp.concatenate(parts, axis=0).T

    def leave(s, carry):
        p = scatter.pair(s)
        rows = rows_at(p * PAIR, PAIR)
        cs, sn = cos[rows], sin[rows]
        gq = (rope_back(dq[rows] * HD**-0.5, cs, sn)).astype(bf16)
        gk = rope_back(dk[rows], cs, sn).astype(bf16)
        gv = dv[rows].astype(bf16)
        mixed = jnp.concatenate([gq, gk, gv], axis=1)
        dlq = nt(mixed, qu[...]).astype(bf16)
        dmix[rows, 0:384] = mixed
        dmix[rows, 384:512] = dlq
        dna = nt(dmix[rows], wq[...])
        x = xf[rows].astype(f32)
        norm_g[0:1, :] += jnp.sum(dna * x, axis=0, keepdims=True)
        norm_g[1:2, :] += jnp.sum(dna, axis=0, keepdims=True)
        scatter.put(s, dna * norm[0:1, :] + dxb[rows])
        scatter.step(s)
        na = (x * norm[0:1, :] + norm[1:2, :]).astype(bf16)
        nb = (x * norm[2:3, :] + norm[3:4, :]).astype(bf16)
        acc_q[...] += tn(dlq, na)
        acc_e[...] += tn(dle[rows], nb)
        return carry

    lax.fori_loop(0, 4, leave, 0)
    up_g = (0.5 * tn(ias[...], db[...])).astype(bf16)
    eu_g = (0.5 * tn(le[...], dpre[...])).astype(bf16)
    sd_g = tn(act[...], dias[:, 128:256]).astype(bf16)
    qd_g, ed_g = acc_q[...].T.astype(bf16), acc_e[...].T.astype(bf16)
    qg = 0.5 * tn(lq[...], dmix[:, 0:384])
    o0, o1, o2 = qg[:, 0:128], pltpu.roll(qg[:, 128:256], HD, 1), qg[:, 256:384]
    low = lax.broadcasted_iota(jnp.int32, o0.shape, 1) < HD
    own_g[0] = jnp.where(low, o0, o1).astype(bf16)
    own_g[1] = jnp.where(low, o2, o0).astype(bf16)
    own_g[2] = jnp.where(low, o1, o2).astype(bf16)
    own_g[3] = tn(att[...], dias[:, 0:128]).astype(bf16)
    for i in range(4):
        own_g[4 + i] = eu_g[:, i * 128 : i * 128 + 128]
        own_g[8 + i] = sd_g[i * 128 : i * 128 + 128, :]
    for i in range(8):
        part = slice(i * 128, i * 128 + 128)
        all_g[i, 0:128] = qd_g[part, :]
        all_g[i, 128:256] = up_g[0:128, part]
        all_g[i, 256:384] = ed_g[part, :]
        all_g[i, 384:512] = up_g[128:256, part]
        norm_o[i] = norm_g[:, part]
    xhat, rstd = centred_rows(stream[...])
    dx = scatter.finish()
    mean_dx = jnp.mean(dx, axis=-1, keepdims=True)
    mean_dxx = jnp.mean(dx * xhat, axis=-1, keepdims=True)
    new_grad[...] = grad[...] + rstd * (dx - mean_dx - xhat * mean_dxx)
    gather.finish()


def backward_layer(layer, grad, stream, norm_params, weights, tables, saved):
    return pl.pallas_call(
        backward_kernel,
        grid=(1,),
        in_specs=[plain(PIECE, D), plain(PIECE, D), layer_of(layer, 4, D)]
        + [layer_of(layer, *s) for s in WEIGHT_SHAPES]
        + [plain(LEN, 128), plain(LEN, 128), plain(1, LEN)]
        + [plain(*s.shape) for s in saved],
        out_specs=[plain(PIECE, D), blocks(12, 128), blocks(8, 512), blocks(8, 8)],
        out_shape=[
            jax.ShapeDtypeStruct((PIECE, D), f32),
            jax.ShapeDtypeStruct((12, 128, 128), bf16),
            jax.ShapeDtypeStruct((8, 512, 128), bf16),
            jax.ShapeDtypeStruct((8, 8, 128), f32),
        ],
        scratch_shapes=[
            pltpu.VMEM((8, D), f32),
            pltpu.VMEM((LEN, D), bf16),
            pltpu.VMEM((LEN, 256), bf16),
            pltpu.VMEM((LEN, 128), bf16),
            pltpu.VMEM((LEN, 512), bf16),
            pltpu.VMEM((LEN, 128), bf16),
            pltpu.VMEM((LEN, D), f32),
            pltpu.VMEM((LEN, 128), f32),
            pltpu.VMEM((LEN, 128), f32),
            pltpu.VMEM((LEN, 128), f32),
            pltpu.VMEM((LEN, 512), bf16),
            pltpu.VMEM((128, LEN), bf16),
            pltpu.VMEM((128, D), f32),
            pltpu.VMEM((128, D), f32),
        ]
        + GATHER_SCRATCH
        + SCATTER_SCRATCH,
        compiler_params=pltpu.CompilerParams(
            collective_id=LAYERS + layer, has_side_effects=True, vmem_limit_bytes=VMEM_LIMIT
        ),
        name="backward",
    )(grad, stream, norm_params, *weights, *tables, *saved)


def tables_of(segments):
    start = jnp.sum((segments[None, :] < segments[:, None]).astype(jnp.int32), axis=1)
    offset = (jnp.arange(LEN, dtype=jnp.int32) - start).astype(f32)
    frequency = jnp.exp(jnp.arange(ROT // 2, dtype=f32) * (-2.0 * math.log(10000.0) / ROT))
    phases = offset[:, None] * frequency[None, :]
    c, s = jnp.cos(phases), jnp.sin(phases)
    one, zero = jnp.ones((LEN, HD - ROT), f32), jnp.zeros((LEN, HD - ROT), f32)
    cos = jnp.concatenate([c, c, one, c, c, one], axis=1)
    sin = jnp.concatenate([s, s, zero, s, s, zero], axis=1)
    return cos, sin, start[None, :]


def block_homes():
    member, place, kind, first, second = [], [], [], [], []
    counts = (8, 24, 8, 8, 8, 32, 32, 8)
    for layer in range(LAYERS):
        for k, count in enumerate(counts):
            for i in range(count):
                each = count // 8
                j = {0: 12, 1: i % 3, 2: 3, 3: 13, 4: 14, 5: 4 + i % 4, 6: 8 + i % 4, 7: 15}[k]
                y, x = j // 4, j % 4
                member.append(i // each)
                place.append(x * 4 + y if layer == 0 else 16 + y * 4 + x)
                kind.append(k)
                first.append(layer)
                second.append(i)
    return [np.array(v, np.int32) for v in (member, place, kind, first, second)]


HOME_MEMBER, HOME_PLACE, BLOCK_KIND, BLOCK_LAYER, BLOCK_INDEX = block_homes()
KIND_COUNT = (8, 24, 8, 8, 8, 32, 32, 8)
KIND_START = (0, 8, 32, 40, 48, 56, 88, 120)
SLOTS = 3


def pick_kernel(kind, layer, idx, *refs):
    s = pl.program_id(0)
    out = refs[-1]
    out[...] = jnp.zeros_like(out)
    for k in range(8):

        @pl.when(kind[s] == k)
        def _(k=k):
            out[...] = refs[k][...]


def pick_weights(kind, layer, idx, adapters):
    def spec(k):
        def where(s, kinds, layers, idxs):
            hit = kinds[s] == k
            i = jnp.where(hit, idxs[s], 0)
            l = jnp.where(hit, layers[s], 0)
            return (l, 0, i) if k % 2 == 1 else (l, i, 0)

        return pl.BlockSpec((None, RANK, RANK), where)

    return pl.pallas_call(
        pick_kernel,
        grid_spec=pltpu.PrefetchScalarGridSpec(
            num_scalar_prefetch=3,
            grid=(SLOTS,),
            in_specs=[spec(k) for k in range(8)],
            out_specs=pl.BlockSpec((None, RANK, RANK), lambda s, a, b, c: (s, 0, 0)),
        ),
        out_shape=jax.ShapeDtypeStruct((SLOTS, RANK, RANK), f32),
        name="pick",
    )(kind, layer, idx, *adapters)


class Axis:
    def __init__(self, name):
        dp, mp = lax.axis_index("dp"), lax.axis_index("mp")
        y, x, z, c = dp // 4, dp % 4, mp // 2, mp % 2
        self.pos = {"x": x, "y": y, "z": z}[name]
        self.plus, self.minus, self.opp = (self.pos + 1) % 4, (self.pos + 3) % 4, (self.pos + 2) % 4

        def device(p):
            if name == "x":
                return {"dp": y * 4 + p}
            if name == "y":
                return {"dp": p * 4 + x}
            return {"mp": p * 2 + c}

        self.up, self.down = device(self.plus), device(self.minus)


def copy_to(src, dst, ssem, rsem, device):
    return pltpu.make_async_remote_copy(
        src_ref=src, dst_ref=dst, send_sem=ssem, recv_sem=rsem, device_id=device, device_id_type=MESH
    )


class AxisGather:
    def __init__(self, axis, buf, rows, split, ssem, rsem):
        self.axis, self.buf, self.ssem, self.rsem = axis, buf, ssem, rsem
        self.halves = (pl.ds(0, split), pl.ds(split, rows - split))

    def cp(self, k, half, sem, device):
        ref = self.buf(k).at[self.halves[half]]
        return copy_to(ref, ref, self.ssem.at[sem], self.rsem.at[sem], device)

    def start(self):
        a = self.axis
        self.cp(a.pos, 0, 0, a.up).start()
        self.cp(a.pos, 1, 1, a.down).start()
        self.cp(a.pos, 1, 2, a.up).start()
        self.cp(a.pos, 0, 3, a.down).start()

    def forward(self, on=None):
        a = self.axis
        self.cp(a.minus, 0, 0, a.up).wait_recv()
        self.cp(a.minus, 0, 4, a.up).start()
        self.cp(a.plus, 1, 1, a.down).wait_recv()
        self.cp(a.plus, 1, 5, a.down).start()
        if on is not None:
            on(0, self.buf(a.minus).at[self.halves[0]])
            on(1, self.buf(a.plus).at[self.halves[1]])

    def wait(self, on=None):
        a = self.axis
        for n, (k, half, sem) in enumerate(((a.minus, 1, 2), (a.plus, 0, 3), (a.opp, 0, 4), (a.opp, 1, 5))):
            self.cp(k, half, sem, a.up).wait_recv()
            if on is not None:
                on(2 + n, self.buf(k).at[self.halves[half]])

    def finish(self):
        a = self.axis
        for half, sem in ((0, 0), (1, 1), (1, 2), (0, 3), (0, 4), (1, 5)):
            self.cp(a.pos, half, sem, a.up).wait_send()


class AxisScatter:
    def __init__(self, axis, terms, rows, split, tr, fin, ssem, rsem):
        self.axis, self.terms, self.tr, self.fin, self.ssem, self.rsem = axis, terms, tr, fin, ssem, rsem
        self.halves = (pl.ds(0, split), pl.ds(split, rows - split))
        self.sizes = (split, rows - split)

    def copies(self):
        a, t, (h0, h1) = self.axis, self.terms, self.halves
        n0, n1 = self.sizes
        return (
            (t(a.opp).at[h0], self.tr.at[0, pl.ds(0, n0)], 0, a.up),
            (t(a.opp).at[h1], self.tr.at[1, pl.ds(0, n1)], 1, a.down),
            (t(a.plus).at[h1], self.fin.at[0, h1], 2, a.up),
            (t(a.minus).at[h0], self.fin.at[1, h0], 3, a.down),
            (t(a.plus).at[h0], self.fin.at[0, h0], 4, a.up),
            (t(a.minus).at[h1], self.fin.at[1, h1], 5, a.down),
        )

    def cp(self, n):
        src, dst, sem, device = self.copies()[n]
        return copy_to(src, dst, self.ssem.at[sem], self.rsem.at[sem], device)

    def start(self):
        for n in range(4):
            self.cp(n).start()

    def middle(self):
        for n in range(2):
            self.cp(n).wait_recv()
            k = (self.axis.plus, self.axis.minus)[n]
            part = self.terms(k).at[self.halves[n]]
            part[...] = (part[...].astype(f32) + self.tr[n, 0 : self.sizes[n]].astype(f32)).astype(bf16)
            self.cp(4 + n).start()

    def total(self):
        for n in range(2, 6):
            self.cp(n).wait_recv()
        return self.terms(self.axis.pos)[...].astype(f32) + self.fin[0].astype(f32) + self.fin[1].astype(f32)

    def finish(self):
        for n in range(6):
            self.cp(n).wait_send()


class MemberScatter:
    def __init__(self, ring, axis, terms, rows, split, prt, mid, tr, fin, psem, qsem, ssem, rsem):
        self.ring, self.terms, self.prt, self.mid, self.psem, self.qsem = ring, terms, prt, mid, psem, qsem
        self.inner = AxisScatter(axis, lambda k: mid.at[k], rows, split, tr, fin, ssem, rsem)
        self.order = (axis.opp, axis.plus, axis.minus, axis.pos)

    def to_partner(self, n):
        r, k = self.ring, self.order[n]
        return copy_to(
            self.terms.at[2 * k + 1 - r.c], self.prt.at[n], self.psem.at[n], self.qsem.at[n], {"mp": r.O}
        )

    def start(self):
        for n in range(4):
            self.to_partner(n).start()

    def add(self, n):
        self.to_partner(n).wait_recv()
        k = self.order[n]
        own = self.terms[2 * k + self.ring.c].astype(f32)
        self.mid[k] = (own + self.prt[n].astype(f32)).astype(bf16)

    def run(self):
        a = self.inner
        self.add(0)
        a.cp(0).start()
        a.cp(1).start()
        self.add(1)
        a.cp(2).start()
        self.add(2)
        a.cp(3).start()
        a.middle()
        self.add(3)
        return a.total()

    def finish(self):
        for n in range(4):
            self.to_partner(n).wait_send()
        self.inner.finish()


LIST_ROWS, LIST_SPLIT = 16 + 8 * 128, 16 + 4 * 128
ROWS_A, ROWS_B = 16 + 4 * 128, 4 * 128
SLOT_ROWS = SLOTS * 128


def update_kernel(
    chosen, own0, own1, all0, all1, norm0, norm1, weights, left_old, right_old, left_root, right_root,
    grad_o, left_o, right_o, norm_o, full_o,
    terms, prt, mid, tr, fin, a1, a1t, a1f, b1, b1t, b1f, a2, a2t, a2f, b2, b2t, b2f, lists,
    terms2, prt2, mid2, tr2, fin2, full, norm_full,
    mp_p, mp_q, mp_s, mp_r, ax_s, ax_r, mp2_p, mp2_q, mp2_s, mp2_r, ag_s, ag_r, pair_s, pair_r, nm_s, nm_r, osem,
):
    ring = Ring()
    ax, ay, az = Axis("x"), Axis("y"), Axis("z")
    for i in range(8):
        terms[i, 0:16] = jnp.concatenate([norm0[i], norm1[i]], axis=0).astype(bf16)
        terms[i, 16:LIST_SPLIT] = all0[i]
        terms[i, LIST_SPLIT:LIST_ROWS] = all1[i]
    barrier = pltpu.get_barrier_semaphore()
    for device in (ax.up, ax.down, ay.up, ay.down, {"mp": ring.R}, {"mp": ring.L}, {"mp": ring.O}):
        pl.semaphore_signal(barrier, inc=1, device_id=device, device_id_type=MESH)
    pl.semaphore_wait(barrier, 7)

    over_mp = MemberScatter(ring, az, terms, LIST_ROWS, LIST_SPLIT, prt, mid, tr, fin, mp_p, mp_q, mp_s, mp_r)
    over_mp.start()
    for j in range(12):
        y, x = j // 4, j % 4
        a1[x, 16 + y * 128 : 144 + y * 128] = own0[j]
        b1[y, x * 128 : x * 128 + 128] = own1[j]
    summed = over_mp.run()
    for j in range(12, 16):
        y, x = j // 4, j % 4
        at = 16 + (j - 12) * 128
        a1[x, 16 + y * 128 : 144 + y * 128] = summed[at : at + 128].astype(bf16)
        b1[y, x * 128 : x * 128 + 128] = summed[at + 512 : at + 640].astype(bf16)
    for x in range(4):
        a1[x, 0:16] = summed[0:16].astype(bf16)
    sa1 = AxisScatter(ax, lambda k: a1.at[k], ROWS_A, 272, a1t, a1f, ax_s.at[0], ax_r.at[0])
    sb1 = AxisScatter(ay, lambda k: b1.at[k], ROWS_B, 256, b1t, b1f, ax_s.at[1], ax_r.at[1])
    sa1.start()
    sb1.start()
    sa1.middle()
    sb1.middle()
    got = sa1.total()
    for y in range(4):
        a2[y, 0:16] = got[0:16].astype(bf16)
        a2[y, 16:144] = got[16 + y * 128 : 144 + y * 128].astype(bf16)
    sa2 = AxisScatter(ay, lambda k: a2.at[k], 144, 80, a2t, a2f, ax_s.at[2], ax_r.at[2])
    sa2.start()
    got = sb1.total()
    for x in range(4):
        b2[x] = got[x * 128 : x * 128 + 128].astype(bf16)
    sb2 = AxisScatter(ax, lambda k: b2.at[k], 128, 64, b2t, b2f, ax_s.at[3], ax_r.at[3])
    sb2.start()
    sa2.middle()
    sb2.middle()

    got = sa2.total()
    x, y = ax.pos, ay.pos
    lists[x * 4 + y] = got[16:144].astype(bf16)
    norm_full[pl.ds(pl.multiple_of(ring.me * 16, 16), 16)] = got[0:16]
    ga1 = AxisGather(ay, lambda k: lists.at[x * 4 + k], 128, 64, ax_s.at[4], ax_r.at[4])
    ga1.start()
    lists[16 + y * 4 + x] = sb2.total().astype(bf16)
    gb1 = AxisGather(ax, lambda k: lists.at[16 + y * 4 + k], 128, 64, ax_s.at[5], ax_r.at[5])
    gb1.start()
    norms = Gather(ring, norm_full, nm_s, nm_r, 16)
    norms.start()
    ga1.forward()
    gb1.forward()
    ga1.wait()
    wide = lists.reshape(8, 4 * 128, 128)
    ga2 = AxisGather(ax, lambda k: wide.at[k], 512, 256, ax_s.at[6], ax_r.at[6])
    ga2.start()
    gb1.wait()
    gb2 = AxisGather(ay, lambda k: wide.at[4 + k], 512, 256, ax_s.at[7], ax_r.at[7])
    gb2.start()
    for s in range(4):
        norms.step_now(s)
    ga2.forward()
    gb2.forward()
    ga2.wait()
    gb2.wait()

    for t in range(8 * SLOTS):
        at = chosen[0, t]
        here = jnp.where(at >= 0, 1.0, 0.0).astype(bf16)
        terms2[t // SLOTS, (t % SLOTS) * 128 : (t % SLOTS) * 128 + 128] = lists[jnp.maximum(at, 0)] * here
    to_slots = MemberScatter(
        ring, az, terms2, SLOT_ROWS, SLOT_ROWS // 2, prt2, mid2, tr2, fin2, mp2_p, mp2_q, mp2_s, mp2_r
    )
    to_slots.start()
    own = to_slots.run()
    c = ring.c
    places = ((az, ax, ay), (ax, ay, az), (ay, az, ax))
    for j in range(SLOTS):
        g = own[j * 128 : j * 128 + 128]
        gl = g.astype(bf16)
        grad_o[j] = g
        scale = (1 - STAT_DECAY) / (jnp.mean(g * g) + STEP_EPS)
        left_o[j] = STAT_DECAY * left_old[j] + nt(gl, gl) * scale
        right_o[j] = STAT_DECAY * right_old[j] + tn(gl, gl) * scale
        way = nn(left_root[j].astype(bf16), gl).astype(bf16)
        way = nn(way, right_root[j].astype(bf16))
        w = weights[j]
        size = jnp.sqrt(jnp.mean(w * w) + STEP_EPS) * lax.rsqrt(jnp.mean(way * way) + STEP_EPS)
        first, second, third = places[j]
        full[j, c, third.pos, second.pos, first.pos] = (w - ADAPT_RATE * size * way).astype(bf16)

    stages = []
    for j in range(SLOTS):
        first, second, third = places[j]
        t, u = third.pos, second.pos
        seconds = full.at[j, c].reshape(4, 4, 512, 128)
        thirds = full.at[j, c].reshape(4, 2048, 128)
        stages.append(
            (
                AxisGather(first, lambda k, j=j, t=t, u=u: full.at[j, c, t, u, k], 128, 64, ag_s.at[0, j], ag_r.at[0, j]),
                AxisGather(second, lambda k, r=seconds, t=t: r.at[t, k], 512, 256, ag_s.at[1, j], ag_r.at[1, j]),
                AxisGather(third, lambda k, r=thirds: r.at[k], 2048, 1024, ag_s.at[2, j], ag_r.at[2, j]),
            )
        )
    partner = {"mp": ring.O}

    def to_partner(j, n, ref):
        copy_to(ref, ref, pair_s.at[j, n], pair_r.at[j, n], partner).start()

    for stage in range(3):
        for j in range(SLOTS):
            stages[j][stage].start()
        for j in range(SLOTS):
            if stage == 2:
                to_partner(j, 6, stages[j][2].buf(places[j][2].pos))
        for j in range(SLOTS):
            stages[j][stage].forward(partial(to_partner, j) if stage == 2 else None)
        for j in range(SLOTS):
            stages[j][stage].wait(partial(to_partner, j) if stage == 2 else None)
    saves = [pltpu.make_async_copy(full.at[j, c], full_o.at[j, c], osem.at[0, j]) for j in range(SLOTS)]
    for save in saves:
        save.start()
    for j in range(SLOTS):
        theirs = full.at[j, 1 - c].reshape(4, 2048, 128)
        for n in range(7):
            part = theirs.at[0] if n == 6 else theirs.at[0, pl.ds(0, 1024)]
            copy_to(part, part, pair_s.at[j, n], pair_r.at[j, n], partner).wait_recv()
    more = [pltpu.make_async_copy(full.at[j, 1 - c], full_o.at[j, 1 - c], osem.at[1, j]) for j in range(SLOTS)]
    for save in more:
        save.start()
    norm_o[...] = norm_full[...]
    for j in range(SLOTS):
        mine = full.at[j, c].reshape(4, 2048, 128)
        for n in range(7):
            part = mine.at[0] if n == 6 else mine.at[0, pl.ds(0, 1024)]
            copy_to(part, part, pair_s.at[j, n], pair_r.at[j, n], partner).wait_send()
        for stage in range(3):
            stages[j][stage].finish()
    for it in (over_mp, to_slots, sa1, sb1, sa2, sb2, ga1, gb1, ga2, gb2, norms):
        it.finish()
    for save in saves + more:
        save.wait()


def update(chosen, own, every, norms, weights, stats):
    one = jax.ShapeDtypeStruct((SLOTS, RANK, RANK), f32)
    dma = pltpu.SemaphoreType.DMA

    def scatter_scratch(rows, split):
        return [pltpu.VMEM((4, rows, 128), bf16), pltpu.VMEM((2, split, 128), bf16), pltpu.VMEM((2, rows, 128), bf16)]

    def member_scratch(rows, split):
        return [pltpu.VMEM((8, rows, 128), bf16), pltpu.VMEM((4, rows, 128), bf16)] + scatter_scratch(rows, split)

    return pl.pallas_call(
        update_kernel,
        in_specs=[pl.BlockSpec(memory_space=pltpu.SMEM)] + vmem_specs(11),
        out_specs=vmem_specs(4) + [pl.BlockSpec(memory_space=pl.ANY)],
        out_shape=[one, one, one, jax.ShapeDtypeStruct((128, 128), f32)]
        + [jax.ShapeDtypeStruct((SLOTS, 2, 4, 4, 4, 128, 128), bf16)],
        scratch_shapes=member_scratch(LIST_ROWS, LIST_SPLIT)
        + scatter_scratch(ROWS_A, 272)
        + scatter_scratch(ROWS_B, 256)
        + scatter_scratch(144, 80)
        + scatter_scratch(128, 64)
        + [pltpu.VMEM((32, 128, 128), bf16)]
        + member_scratch(SLOT_ROWS, SLOT_ROWS // 2)
        + [pltpu.VMEM((SLOTS, 2, 4, 4, 4, 128, 128), bf16), pltpu.VMEM((128, 128), f32)]
        + [dma((4,)), dma((4,)), dma((6,)), dma((6,)), dma((8, 6)), dma((8, 6))]
        + [dma((4,)), dma((4,)), dma((6,)), dma((6,)), dma((3, 3, 6)), dma((3, 3, 6))]
        + [dma((3, 7)), dma((3, 7)), dma((13,)), dma((13,)), dma((2, 3))],
        compiler_params=pltpu.CompilerParams(
            collective_id=2 * LAYERS, has_side_effects=True, vmem_limit_bytes=VMEM_LIMIT
        ),
        name="update",
    )(chosen, own[0], own[1], every[0], every[1], norms[0], norms[1], weights, *stats)


def unpack_kernel(place, full, *outs):
    t = pl.program_id(0)
    layer, i = t // 8, t % 8
    for k in range(8):
        each = KIND_COUNT[k] // 8
        for n in range(each):
            block = full[place[layer * 128 + KIND_START[k] + i * each + n]].astype(f32)
            if k % 2 == 1:
                outs[k][:, n * 128 : n * 128 + 128] = block
            else:
                outs[k][n * 128 : n * 128 + 128, :] = block


def unpack(place, full):
    def spec(k):
        each = KIND_COUNT[k] // 8
        if k % 2 == 1:
            return pl.BlockSpec((None, RANK, each * RANK), lambda t, p: (t // 8, 0, t % 8))
        return pl.BlockSpec((None, each * RANK, RANK), lambda t, p: (t // 8, t % 8, 0))

    shapes = [(LAYERS, RANK, c * RANK) if k % 2 == 1 else (LAYERS, c * RANK, RANK) for k, c in enumerate(KIND_COUNT)]
    return pl.pallas_call(
        unpack_kernel,
        grid_spec=pltpu.PrefetchScalarGridSpec(
            num_scalar_prefetch=1,
            grid=(8 * LAYERS,),
            in_specs=[pl.BlockSpec(memory_space=pltpu.VMEM)],
            out_specs=[spec(k) for k in range(8)],
        ),
        out_shape=[jax.ShapeDtypeStruct(s, f32) for s in shapes],
        compiler_params=pltpu.CompilerParams(vmem_limit_bytes=VMEM_LIMIT),
        name="unpack",
    )(place, full)


def slot_plan(owner_slot):
    dp, mp = lax.axis_index("dp"), lax.axis_index("mp")
    mine = lax.broadcasted_iota(jnp.int32, (8 * SLOTS, 256), 0) + dp * (8 * SLOTS)
    hit = mine == owner_slot[None, :]
    here = hit & (jnp.asarray(HOME_MEMBER)[None, :] == mp)
    chosen = jnp.sum(jnp.where(here, jnp.asarray(HOME_PLACE)[None, :] + 1, 0), axis=1) - 1
    own = lax.broadcasted_iota(jnp.int32, (SLOTS, 256), 0) + (dp * (8 * SLOTS) + mp * SLOTS) == owner_slot[None, :]

    def of(table, base):
        return jnp.sum(jnp.where(own, jnp.asarray(table)[None, :] - base, 0), axis=1) + base

    j, device = owner_slot % SLOTS, owner_slot // SLOTS
    y, x, z, c = device // 32, device // 8 % 4, device % 8 // 2, device % 2
    orders = (y * 16 + x * 4 + z, z * 16 + y * 4 + x, x * 16 + z * 4 + y)
    inner = jnp.where(j == 0, orders[0], jnp.where(j == 1, orders[1], orders[2]))
    place = (j * 2 + c) * 64 + inner
    return chosen[None, :], (of(BLOCK_KIND, -1), of(BLOCK_LAYER, 0), of(BLOCK_INDEX, 0)), place


def body(
    hidden_in, cotangent, segments, qkv_weight, out_weight, up_weight, down_weight,
    query_down, query_up, output_down, output_up, expand_down, expand_up, shrink_down, shrink_up,
    norm_params, norm_first, norm_second, owner_slot, left_stats, right_stats, left_roots, right_roots,
):
    adapters = (query_down, query_up, output_down, output_up, expand_down, expand_up, shrink_down, shrink_up)
    member = lax.axis_index("mp")
    tables = tables_of(segments)
    chosen, own_blocks, place = slot_plan(owner_slot)
    own_weights = pick_weights(*own_blocks, adapters)
    prepared = prepare(
        member.astype(jnp.int32)[None], qkv_weight, query_down, query_up, output_down, output_up,
        expand_down, expand_up, shrink_down, shrink_up,
    )
    weights = tuple(prepared) + (up_weight, down_weight, out_weight)
    streams, kept = [hidden_in.astype(f32)], []
    for layer in range(LAYERS):
        made = forward_layer(layer, streams[-1], norm_params, weights, tables)
        streams.append(made[0])
        kept.append(made[1:])
    grad = cotangent
    own, every, norms = [None] * LAYERS, [None] * LAYERS, [None] * LAYERS
    for layer in reversed(range(LAYERS)):
        grad, own[layer], every[layer], norms[layer] = backward_layer(
            layer, grad, streams[layer], norm_params, weights, tables, kept[layer]
        )
    stats = (left_stats, right_stats, left_roots, right_roots)
    slot_grads, left_new, right_new, norm_sums, full = update(chosen, own, every, norms, own_weights, stats)
    renewed = unpack(place, full.reshape(2 * 64 * SLOTS, RANK, RANK))
    grad_norm = norm_sums.reshape(8, LAYERS, 8, 128)[:, :, :4].transpose(1, 2, 0, 3).reshape(LAYERS, 4, D)
    moment = MOMENT_DECAY * norm_first + (1 - MOMENT_DECAY) * grad_norm
    square = SQUARE_DECAY * norm_second + (1 - SQUARE_DECAY) * grad_norm * grad_norm
    renewed_norms = norm_params - NORM_RATE * (moment / (1 - MOMENT_DECAY**ADAM_STEP)) / (
        jnp.sqrt(square / (1 - SQUARE_DECAY**ADAM_STEP)) + ADAM_EPS
    )
    return (
        streams[-1], grad, slot_grads, left_new, right_new, *renewed,
        moment, square[:, :2], square[:, 2:], renewed_norms,
    )


def solution(mesh):
    both = P(("dp", "mp"))
    cols, rows, copied = P(None, None, "mp"), P(None, "mp", None), P()
    in_specs = (both, both, P("dp"), cols, rows, cols, rows) + (copied,) * 12 + (both,) * 4
    out_specs = (both,) * 5 + (copied,) * 12
    return jax.shard_map(body, mesh=mesh, in_specs=in_specs, out_specs=out_specs, check_vma=False)
```

```python
from functools import partial
import math

import jax
import jax.numpy as jnp
import numpy as np
from jax import lax
from jax.experimental import pallas as pl
from jax.experimental.pallas import tpu as pltpu
from jax.sharding import PartitionSpec as P

D = 1024
HD = 64
FF = 4096
ROT = 16
RANK = 128
LAYERS = 2
LEN = 1024
PIECE = 128
PAIR = 256
HALF = 64
ADAM_STEP = 10
NORM_EPS = 1e-05
STAT_DECAY = 0.9
ADAPT_RATE = 0.4
STEP_EPS = 1e-06
MOMENT_DECAY = 0.9
SQUARE_DECAY = 0.95
NORM_RATE = 1.0
ADAM_EPS = 1e-08
MASKED = -1e30

MESH = pl.DeviceIdType.MESH
f32 = jnp.float32
bf16 = jnp.bfloat16
VMEM_LIMIT = 56 * 2**20


def nn(a, b):
    return lax.dot_general(a, b, (((1,), (0,)), ((), ())), preferred_element_type=f32)


def nt(a, b):
    return lax.dot_general(a, b, (((1,), (1,)), ((), ())), preferred_element_type=f32)


def tn(a, b):
    return lax.dot_general(a, b, (((0,), (0,)), ((), ())), preferred_element_type=f32)


def fill_tables(seg, cos_o, sin_o, start_o):
    pos = lax.broadcasted_iota(jnp.int32, (8, LEN), 1)
    numbers = jnp.broadcast_to(seg[...], (8, LEN))
    start = jnp.where(numbers != pltpu.roll(numbers, 1, 1), pos, 0)
    for n in range(10):
        start = jnp.maximum(start, jnp.where(pos >= 2**n, pltpu.roll(start, 2**n, 1), 0))
    start_o[...] = start[0:1, :]
    row = lax.broadcasted_iota(jnp.int32, (8, LEN), 0).astype(f32)
    phases = (pos - start).astype(f32) * jnp.exp(row * (-2.0 * math.log(10000.0) / ROT))
    c, s = jnp.cos(phases), jnp.sin(phases)
    one, zero = jnp.ones((HD - ROT, LEN), f32), jnp.zeros((HD - ROT, LEN), f32)
    cos_o[...] = jnp.concatenate([c, c, one, c, c, one], axis=0).T
    sin_o[...] = jnp.concatenate([s, s, zero, s, s, zero], axis=0).T


def prep_kernel(
    plan, qkv, qd, qu, od, ou, ed, eu, sd, su, seg, *rest
):
    homes, (wq_o, qu_o, od_o, oush_o, ed_o, eu_o, sd_o, home_o, cos_o, sin_o, start_o) = rest[:8], rest[8:]
    for k in range(8):

        @pl.when(plan[2 + plan[0]] == k)
        def _(k=k):
            home_o[...] = homes[k][...]

    pl.when(pl.program_id(0) == 0)(partial(fill_tables, seg, cos_o, sin_o, start_o))

    def regroup(groups):
        low = lax.broadcasted_iota(jnp.int32, groups[0].shape, 1) < HD
        return (
            jnp.where(low, groups[0], groups[1]),
            pltpu.roll(jnp.where(low, groups[2], groups[0]), HD, 1),
            jnp.where(low, groups[1], groups[2]),
        )

    for i, part in enumerate(regroup([qkv[:, i * 128 : i * 128 + 128].astype(f32) for i in range(3)])):
        wq_o[:, i * 128 : i * 128 + 128] = part.astype(bf16)
    wq_o[:, 384:512] = qd[...].astype(bf16)
    for i, part in enumerate(regroup([qu[:, i * 128 : i * 128 + 128] for i in range(3)])):
        qu_o[:, i * 128 : i * 128 + 128] = (0.5 * part).astype(bf16)
    od_o[...] = od[...].astype(bf16)
    oush_o[0:128, :] = (0.5 * ou[...]).astype(bf16)
    oush_o[128:256, :] = (0.5 * su[...]).astype(bf16)
    ed_o[...] = ed[...].astype(bf16)
    eu_o[...] = (0.5 * eu[...]).astype(bf16)
    sd_o[...] = sd[...].astype(bf16)


def prepare(plan, segments, qkv, adapters):
    qd, qu, od, ou, ed, eu, sd, su = adapters

    def whole(rows, cols):
        return pl.BlockSpec((None, rows, cols), lambda l, p: (l, 0, 0))

    def by_cols(rows, cols):
        return pl.BlockSpec((None, rows, cols), lambda l, p: (l, 0, p[1]))

    def by_rows(rows, cols):
        return pl.BlockSpec((None, rows, cols), lambda l, p: (l, p[1], 0))

    def home(k):
        def where(l, p):
            i = jnp.where(p[2 + p[0]] == k, p[1] * p[18 + p[0]] + p[34 + p[0]], 0)
            return (l, 0, i) if k % 2 == 1 else (l, i, 0)

        return pl.BlockSpec((None, RANK, RANK), where)

    def once(rows, cols):
        return pl.BlockSpec((rows, cols), lambda l, p: (0, 0))

    shapes = [(1024, 512), (128, 384), (128, 128), (256, 1024), (1024, 128), (128, 512), (512, 128)]
    return pl.pallas_call(
        prep_kernel,
        grid_spec=pltpu.PrefetchScalarGridSpec(
            num_scalar_prefetch=1,
            grid=(LAYERS,),
            in_specs=[
                whole(1024, 384),
                whole(1024, 128),
                by_cols(128, 384),
                by_rows(128, 128),
                whole(128, 1024),
                whole(1024, 128),
                by_cols(128, 512),
                by_rows(512, 128),
                whole(128, 1024),
                once(1, LEN),
            ]
            + [home(k) for k in range(8)],
            out_specs=[whole(*s) for s in shapes]
            + [whole(RANK, RANK), once(LEN, 128), once(LEN, 128), once(1, LEN)],
        ),
        out_shape=[jax.ShapeDtypeStruct((LAYERS,) + s, bf16) for s in shapes]
        + [
            jax.ShapeDtypeStruct((LAYERS, RANK, RANK), f32),
            jax.ShapeDtypeStruct((LEN, 128), f32),
            jax.ShapeDtypeStruct((LEN, 128), f32),
            jax.ShapeDtypeStruct((1, LEN), jnp.int32),
        ],
        compiler_params=pltpu.CompilerParams(vmem_limit_bytes=VMEM_LIMIT),
        name="prep",
    )(plan, qkv, qd, qu, od, ou, ed, eu, sd, su, segments[None, :], *adapters)


class Ring:
    def __init__(self):
        me = lax.axis_index("mp")
        z, c = me // 2, me % 2
        self.me, self.z, self.c = me, z, c
        self.zp, self.zm, self.z2 = (z + 1) % 4, (z + 3) % 4, (z + 2) % 4
        self.R, self.L, self.O = 2 * self.zp + c, 2 * self.zm + c, 2 * z + 1 - c

    def greet(self):
        barrier = pltpu.get_barrier_semaphore()
        for i in (self.R, self.L, self.O):
            pl.semaphore_signal(barrier, inc=1, device_id={"mp": i}, device_id_type=MESH)
        pl.semaphore_wait(barrier, 3)


def rcopy(src, dst, ssem, rsem, to):
    return pltpu.make_async_remote_copy(
        src_ref=src, dst_ref=dst, send_sem=ssem, recv_sem=rsem, device_id={"mp": to}, device_id_type=MESH
    )


def rows_at(start, size):
    return pl.ds(pl.multiple_of(start, size), size)


class Gather:
    def __init__(self, ring, full, ssem, rsem, piece=PIECE):
        self.ring, self.full, self.ssem, self.rsem = ring, full, ssem, rsem
        self.piece = piece

    def cp(self, idx, half, sem, to):
        if half is None:
            sl = rows_at(idx * self.piece, self.piece)
        else:
            sl = rows_at(idx * self.piece + half * (self.piece // 2), self.piece // 2)
        return rcopy(self.full.at[sl], self.full.at[sl], self.ssem.at[sem], self.rsem.at[sem], to)

    def start(self):
        r = self.ring
        self.cp(r.me, 0, 0, r.R).start()
        self.cp(r.me, 1, 1, r.L).start()
        self.cp(r.me, None, 6, r.O).start()
        self.cp(r.me, 1, 2, r.R).start()
        self.cp(r.me, 0, 3, r.L).start()

    def step(self, s):
        for n in range(4):
            pl.when(s == n)(partial(self.step_now, n))

    def step_now(self, n):
        r, cp = self.ring, self.cp
        O, R, L = r.O, r.R, r.L
        zl, zr, zq = 2 * r.zm + r.c, 2 * r.zp + r.c, 2 * r.z2 + r.c
        pl_, pr_, pq = 2 * r.zm + 1 - r.c, 2 * r.zp + 1 - r.c, 2 * r.z2 + 1 - r.c
        if n == 0:
            cp(O, None, 6, O).wait_recv()
        elif n == 1:
            cp(zl, 0, 0, R).wait_recv()
            cp(zl, 0, 4, R).start()
            cp(zl, 0, 7, O).start()
            cp(zr, 1, 1, L).wait_recv()
            cp(zr, 1, 5, L).start()
            cp(zr, 1, 8, O).start()
            cp(zl, 1, 2, R).wait_recv()
            cp(zl, 1, 9, O).start()
            cp(pl_, 0, 7, O).wait_recv()
            cp(pl_, 1, 9, O).wait_recv()
        elif n == 2:
            cp(zr, 0, 3, L).wait_recv()
            cp(zr, 0, 10, O).start()
            cp(pr_, 1, 8, O).wait_recv()
            cp(pr_, 0, 10, O).wait_recv()
        else:
            cp(zq, 0, 4, R).wait_recv()
            cp(zq, 0, 11, O).start()
            cp(zq, 1, 5, L).wait_recv()
            cp(zq, 1, 12, O).start()
            cp(pq, 0, 11, O).wait_recv()
            cp(pq, 1, 12, O).wait_recv()

    def pair(self, s):
        z = self.ring.z
        return (z + jnp.where(s == 0, 0, jnp.where(s == 1, 3, jnp.where(s == 2, 1, 2)))) % 4

    def finish(self):
        r = self.ring
        for sem in range(13):
            self.cp(r.me, None if sem == 6 else 0, sem, r.O).wait_send()


class Scatter:
    def __init__(self, ring, pb, prt, tr, fin, work, ssem, rsem):
        self.ring, self.pb, self.prt, self.tr, self.fin, self.work = ring, pb, prt, tr, fin, work
        self.ssem, self.rsem = ssem, rsem

    def pair(self, s):
        z = self.ring.z
        return (z + jnp.where(s == 0, 2, jnp.where(s == 1, 1, jnp.where(s == 2, 3, 0)))) % 4

    def cp(self, src, dst, sem, to):
        return rcopy(src, dst, self.ssem.at[sem], self.rsem.at[sem], to)

    def to_partner(self, s):
        r = self.ring
        theirs = self.pb.at[s, rows_at((1 - r.c) * PIECE, PIECE)]
        return self.cp(theirs, self.prt.at[s], s, r.O)

    def put(self, s, term):
        self.pb[s] = term.astype(bf16)
        self.to_partner(s).start()

    def summed(self, s):
        self.to_partner(s).wait_recv()
        own = self.pb[s, rows_at(self.ring.c * PIECE, PIECE)]
        return own.astype(f32) + self.prt[s].astype(f32)

    def h(self, i):
        return pl.ds(i * HALF, HALF)

    def c_tr0(self):
        return self.cp(self.work.at[0, self.h(0)], self.tr.at[0], 4, self.ring.R)

    def c_tr1(self):
        return self.cp(self.work.at[0, self.h(1)], self.tr.at[1], 5, self.ring.L)

    def c_r1(self):
        return self.cp(self.work.at[1, self.h(1)], self.fin.at[0, self.h(1)], 6, self.ring.R)

    def c_l0(self):
        return self.cp(self.work.at[2, self.h(0)], self.fin.at[1, self.h(0)], 7, self.ring.L)

    def c_r0(self):
        return self.cp(self.work.at[1, self.h(0)], self.fin.at[0, self.h(0)], 8, self.ring.R)

    def c_l1(self):
        return self.cp(self.work.at[2, self.h(1)], self.fin.at[1, self.h(1)], 9, self.ring.L)

    def step(self, s):
        for n in range(1, 5):
            pl.when(s == n)(partial(self.step_now, n))

    def step_now(self, n):
        if n == 1:
            self.work[0] = self.summed(0).astype(bf16)
            self.c_tr0().start()
            self.c_tr1().start()
        elif n == 2:
            self.work[1] = self.summed(1).astype(bf16)
            self.c_r1().start()
        elif n == 3:
            self.work[2] = self.summed(2).astype(bf16)
            self.c_l0().start()
            self.pass_on(0)
        else:
            self.pass_on(1)

    def pass_on(self, n):
        h = self.h(n)
        (self.c_tr0, self.c_tr1)[n]().wait_recv()
        self.work[1 + n, h] = (self.work[1 + n, h].astype(f32) + self.tr[n].astype(f32)).astype(bf16)
        (self.c_r0, self.c_l1)[n]().start()

    def finish(self):
        total = self.summed(3)
        self.c_r1().wait_recv()
        self.c_l0().wait_recv()
        self.c_r0().wait_recv()
        self.c_l1().wait_recv()
        total = total + self.fin[0].astype(f32) + self.fin[1].astype(f32)
        for s in range(4):
            self.to_partner(s).wait_send()
        for c in (self.c_tr0, self.c_tr1, self.c_r1, self.c_l0, self.c_r0, self.c_l1):
            c().wait_send()
        return total


GATHER_SCRATCH = [pltpu.SemaphoreType.DMA((13,)), pltpu.SemaphoreType.DMA((13,))]
SCATTER_SCRATCH = [
    pltpu.VMEM((4, PAIR, D), bf16),
    pltpu.VMEM((4, PIECE, D), bf16),
    pltpu.VMEM((2, HALF, D), bf16),
    pltpu.VMEM((2, PIECE, D), bf16),
    pltpu.VMEM((3, PIECE, D), bf16),
    pltpu.SemaphoreType.DMA((10,)),
    pltpu.SemaphoreType.DMA((10,)),
]


def centred_rows(x):
    cen = x - jnp.mean(x, axis=-1, keepdims=True)
    rstd = lax.rsqrt(jnp.mean(cen * cen, axis=-1, keepdims=True) + NORM_EPS)
    return cen * rstd, rstd


def lane_in_head(shape):
    return lax.broadcasted_iota(jnp.int32, shape, 1) % HD


def rope(x, cos, sin):
    lane = lane_in_head(x.shape)
    turned = jnp.where(lane < ROT // 2, -pltpu.roll(x, 128 - ROT // 2, 1), pltpu.roll(x, ROT // 2, 1))
    return x * cos + turned * sin


def rope_back(g, cos, sin):
    lane = lane_in_head(g.shape)
    w = g * sin
    turned = jnp.where(
        lane < ROT // 2,
        pltpu.roll(w, 128 - ROT // 2, 1),
        jnp.where(lane < ROT, -pltpu.roll(w, ROT // 2, 1), 0.0),
    )
    return g * cos + turned


def allowed_keys(start_ref, k):
    keys = PAIR * (k + 1)
    kpos = lax.broadcasted_iota(jnp.int32, (keys, PAIR), 0)
    qpos = lax.broadcasted_iota(jnp.int32, (keys, PAIR), 1) + PAIR * k
    return (kpos >= start_ref[0:1, PAIR * k : PAIR * k + PAIR]) & (kpos <= qpos)


def forward_rows(r, rows):
    x = r.xf[rows].astype(f32)
    na = (x * r.norm[0:1, :] + r.norm[1:2, :]).astype(bf16)
    nb = (x * r.norm[2:3, :] + r.norm[3:4, :]).astype(bf16)
    m = nn(na, r.wq[...])
    lq = m[:, 384:512].astype(bf16)
    r.lq[rows] = lq
    m = m[:, 0:384] + nn(lq, r.qu[...])
    cs, sn = r.cos[rows], r.sin[rows]
    r.q[rows] = (rope(m[:, 0:128], cs, sn) * HD**-0.5).astype(bf16)
    r.k[rows] = rope(m[:, 128:256], cs, sn).astype(bf16)
    v = m[:, 256:384]
    r.v[rows] = v.astype(bf16)
    r.vt[:, rows] = v.T.astype(bf16)
    le = nn(nb, r.ed[...]).astype(bf16)
    r.le[rows] = le
    pre = nn(nb, r.up[...]) + nn(le, r.eu[...])
    cdf = 0.5 + 0.5 * lax.erf(pre * (0.5**0.5))
    act = (pre * cdf).astype(bf16)
    r.act[rows] = act
    r.gp[rows] = (cdf + pre * (jnp.exp(-0.5 * pre * pre) * ((2 * math.pi) ** -0.5))).astype(bf16)
    r.ias[rows, 128:256] = nn(act, r.sd[...]).astype(bf16)


def attend(r, blk):
    keys = PAIR * (blk + 1)
    rows = slice(PAIR * blk, PAIR * blk + PAIR)
    ok = allowed_keys(r.start, blk)
    qp = r.q[rows, :]
    head = lax.broadcasted_iota(jnp.int32, qp.shape, 1) // HD
    parts = []
    for h in range(2):
        qm = jnp.where(head == h, qp, jnp.zeros_like(qp))
        s = jnp.where(ok, nt(r.k[0:keys, :], qm), MASKED)
        top = jnp.max(s, axis=0, keepdims=True)
        e = jnp.exp(s - top)
        total = jnp.sum(e, axis=0, keepdims=True)
        r.lse[h : h + 1, rows] = top + jnp.log(total)
        o = nn(r.vt[h * HD : h * HD + HD, 0:keys], e.astype(bf16))
        parts.append(o / total)
    r.att[rows, :] = jnp.concatenate(parts, axis=0).T.astype(bf16)


def branch_rows(r, rows):
    att = r.att[rows]
    r.ias[rows, 0:128] = nn(att, r.od[...]).astype(bf16)
    return nn(r.act[rows], r.down[...]) + nn(att, r.out_w[...]) + nn(r.ias[rows], r.oush[...])


def backward_rows(r, rows):
    d = r.db[rows]
    di = nt(d, r.oush[...]).astype(bf16)
    r.dias[rows] = di
    r.datt[rows] = (nt(d, r.out_w[...]) + nt(di[:, 0:128], r.od[...])).astype(bf16)
    dact = nt(d, r.down[...]) + nt(di[:, 128:256], r.sd[...])
    dp = (dact * r.gp[rows].astype(f32)).astype(bf16)
    r.dpre[rows] = dp
    dl = nt(dp, r.eu[...]).astype(bf16)
    r.dle[rows] = dl
    dnb = nt(dp, r.up[...]) + nt(dl, r.ed[...])
    x = r.xf[rows].astype(f32)
    r.norm_g[2:3, :] += jnp.sum(dnb * x, axis=0, keepdims=True)
    r.norm_g[3:4, :] += jnp.sum(dnb, axis=0, keepdims=True)
    r.dxb[rows] = dnb * r.norm[2:3, :]


def clear(r):
    for ref in (r.norm_g, r.dk, r.dv, r.acc_q, r.acc_e):
        ref[...] = jnp.zeros_like(ref)


def attend_back(r, blk):
    keys = PAIR * (blk + 1)
    rows = slice(PAIR * blk, PAIR * blk + PAIR)
    ok = allowed_keys(r.start, blk)
    qp, dp = r.q[rows, :], r.datt[rows, :]
    head = lax.broadcasted_iota(jnp.int32, qp.shape, 1) // HD
    parts = []
    for h in range(2):
        qm = jnp.where(head == h, qp, jnp.zeros_like(qp))
        dm = jnp.where(head == h, dp, jnp.zeros_like(dp))
        prob = jnp.where(ok, jnp.exp(nt(r.k[0:keys, :], qm) - r.lse[h : h + 1, rows]), 0.0)
        weighted = prob * nt(r.v[0:keys, :], dm)
        ds = (weighted - prob * jnp.sum(weighted, axis=0, keepdims=True)).astype(bf16)
        r.dv[0:keys, :] += nn(prob.astype(bf16), dm)
        r.dk[0:keys, :] += nn(ds, qm)
        parts.append(nn(r.kt[h * HD : h * HD + HD, 0:keys], ds))
    r.dq[rows, :] = jnp.concatenate(parts, axis=0).T


def stream_grad_rows(r, rows):
    cs, sn = r.cos[rows], r.sin[rows]
    gq = (rope_back(r.dq[rows] * HD**-0.5, cs, sn)).astype(bf16)
    gk = rope_back(r.dk[rows], cs, sn).astype(bf16)
    gv = r.dv[rows].astype(bf16)
    mixed = jnp.concatenate([gq, gk, gv], axis=1)
    r.dmix[rows, 0:384] = mixed
    r.dmix[rows, 384:512] = nt(mixed, r.qu[...]).astype(bf16)
    dna = nt(r.dmix[rows], r.wq[...])
    x = r.xf[rows].astype(f32)
    r.norm_g[0:1, :] += jnp.sum(dna * x, axis=0, keepdims=True)
    r.norm_g[1:2, :] += jnp.sum(dna, axis=0, keepdims=True)
    return dna * r.norm[0:1, :] + r.dxb[rows]


def down_grad_rows(r, rows):
    x = r.xf[rows].astype(f32)
    na = (x * r.norm[0:1, :] + r.norm[1:2, :]).astype(bf16)
    nb = (x * r.norm[2:3, :] + r.norm[3:4, :]).astype(bf16)
    r.acc_q[...] += tn(r.dmix[rows, 384:512], na)
    r.acc_e[...] += tn(r.dle[rows], nb)


def adapter_grads(r, own_g, all_g, norm_o):
    up_g = (0.5 * tn(r.ias[...], r.db[...])).astype(bf16)
    eu_g = (0.5 * tn(r.le[...], r.dpre[...])).astype(bf16)
    sd_g = tn(r.act[...], r.dias[:, 128:256]).astype(bf16)
    qd_g, ed_g = r.acc_q[...].T.astype(bf16), r.acc_e[...].T.astype(bf16)
    qg = 0.5 * tn(r.lq[...], r.dmix[:, 0:384])
    o0, o1, o2 = qg[:, 0:128], pltpu.roll(qg[:, 128:256], HD, 1), qg[:, 256:384]
    low = lax.broadcasted_iota(jnp.int32, o0.shape, 1) < HD
    own_g[0] = jnp.where(low, o0, o1).astype(bf16)
    own_g[1] = jnp.where(low, o2, o0).astype(bf16)
    own_g[2] = jnp.where(low, o1, o2).astype(bf16)
    own_g[3] = tn(r.att[...], r.dias[:, 0:128]).astype(bf16)
    for i in range(4):
        own_g[4 + i] = eu_g[:, i * 128 : i * 128 + 128]
        own_g[8 + i] = sd_g[i * 128 : i * 128 + 128, :]
    for i in range(8):
        part = slice(i * 128, i * 128 + 128)
        all_g[i, 0:128] = qd_g[part, :]
        all_g[i, 128:256] = up_g[0:128, part]
        all_g[i, 256:384] = ed_g[part, :]
        all_g[i, 384:512] = up_g[128:256, part]
        norm_o[i] = r.norm_g[:, part]


def norm_back(stream, dx):
    xhat, rstd = centred_rows(stream)
    mean_dx = jnp.mean(dx, axis=-1, keepdims=True)
    mean_dxx = jnp.mean(dx * xhat, axis=-1, keepdims=True)
    return rstd * (dx - mean_dx - xhat * mean_dxx)


WEIGHTS = ("wq", "qu", "od", "oush", "ed", "eu", "sd", "up", "down", "out_w")
WEIGHT_SHAPES = [(1024, 512), (128, 384), (128, 128), (256, 1024), (1024, 128), (128, 512), (512, 128),
                 (1024, 512), (512, 1024), (128, 1024)]
KEPT = {"xf": (LEN, D), "q": (LEN, 128), "k": (LEN, 128), "v": (LEN, 128), "act": (LEN, 512), "gp": (LEN, 512),
        "lq": (LEN, 128), "le": (LEN, 128), "att": (LEN, 128), "ias": (LEN, 256), "lse": (8, LEN)}
TABLES = {"cos": (LEN, 128), "sin": (LEN, 128)}
BACK = {"db": (LEN, D), "dias": (LEN, 256), "datt": (LEN, 128), "dpre": (LEN, 512), "dle": (LEN, 128),
        "dmix": (LEN, 512), "kt": (128, LEN)}
BACK_WIDE = {"norm_g": (8, D), "dxb": (LEN, D), "dq": (LEN, 128), "dk": (LEN, 128), "dv": (LEN, 128),
             "acc_q": (128, D), "acc_e": (128, D)}


class Refs:
    pass


class Layout:
    def __init__(self):
        self.inputs, self.outputs, self.scratch = [], [], []

    def add_in(self, name, spec, array):
        self.inputs.append((name, spec, array))

    def add_out(self, name, spec, shape, dtype):
        self.outputs.append((name, spec, jax.ShapeDtypeStruct(shape, dtype)))

    def add_scratch(self, name, what):
        self.scratch.append((name, what))

    def add_vmem(self, shapes, dtype):
        for name, shape in shapes.items():
            self.add_scratch(name, pltpu.VMEM(shape, f32 if name in ("lse", "cos", "sin") else dtype))

    def call(self, body, name, collective_id):
        names = [e[0] for e in self.inputs + self.outputs + self.scratch]

        def kernel(*refs):
            r = Refs()
            for key, ref in zip(names, refs):
                setattr(r, key, ref)
            body(r)

        return pl.pallas_call(
            kernel,
            in_specs=[e[1] for e in self.inputs],
            out_specs=[e[1] for e in self.outputs],
            out_shape=[e[2] for e in self.outputs],
            scratch_shapes=[e[1] for e in self.scratch],
            compiler_params=pltpu.CompilerParams(
                collective_id=collective_id, has_side_effects=True, vmem_limit_bytes=VMEM_LIMIT
            ),
            name=name,
        )(*[e[2] for e in self.inputs])


IN_VMEM = pl.BlockSpec(memory_space=pltpu.VMEM)
IN_HBM = pl.BlockSpec(memory_space=pl.ANY)


class Loads:
    def __init__(self, r, layer, kept):
        self.copies = {}
        r.norm = r.norms_in.at[layer]
        names = list(WEIGHTS) + list(TABLES) + list(kept)
        for n, name in enumerate(names):
            src = getattr(r, "hbm_" + name)
            if name in WEIGHTS:
                src = src.at[layer]
            self.copies[name] = pltpu.make_async_copy(src, getattr(r, name), r.load_sem.at[n])

    def start(self, *names):
        for name in names:
            self.copies[name].start()

    def wait(self, *names):
        for name in names:
            self.copies[name].wait()


def add_layer_inputs(lay, norm_params, layer, weights, tables, kept=()):
    lay.add_in("norms_in", IN_VMEM, norm_params)
    for name, array in zip(WEIGHTS, weights):
        lay.add_in("hbm_" + name, IN_HBM, array)
    for name, array in zip(TABLES, tables):
        lay.add_in("hbm_" + name, IN_HBM, array)
    lay.add_in("start", IN_VMEM, tables[2])
    for name, array in zip(KEPT, kept):
        lay.add_in("hbm_" + name, IN_HBM, array)
    lay.add_vmem(dict(zip(WEIGHTS, WEIGHT_SHAPES)), bf16)
    lay.add_vmem(TABLES, f32)
    lay.add_vmem(KEPT, bf16)
    lay.add_scratch("load_sem", pltpu.SemaphoreType.DMA((len(WEIGHTS) + 2 + len(KEPT),)))


def add_gather(lay, name):
    for key, what in zip(("s", "r"), GATHER_SCRATCH):
        lay.add_scratch(name + key, what)


def add_scatter(lay, name):
    for key, what in zip(("pb", "prt", "tr", "fin", "work", "s", "r"), SCATTER_SCRATCH):
        lay.add_scratch(name + key, what)


def scatter_of(r, ring, name):
    return Scatter(ring, *[getattr(r, name + key) for key in ("pb", "prt", "tr", "fin", "work", "s", "r")])


FIRST_LOADS = ("wq", "qu", "cos", "sin", "ed", "up", "eu", "sd")
LATER_LOADS = ("down", "out_w", "od", "oush")


def first_body(r):
    ring = Ring()
    gather = Gather(ring, r.xf, r.gxs, r.gxr)
    scatter = scatter_of(r, ring, "sf")
    loads = Loads(r, 0, ())
    loads.start(*FIRST_LOADS, *LATER_LOADS)
    r.xf[rows_at(ring.me * PIECE, PIECE)] = centred_rows(r.stream[...].astype(f32))[0].astype(bf16)
    ring.greet()
    gather.start()
    loads.wait(*FIRST_LOADS)

    def arrive(s, carry):
        gather.step(s)
        forward_rows(r, rows_at(gather.pair(s) * PAIR, PAIR))
        return carry

    lax.fori_loop(0, 4, arrive, 0)

    def save(name, n):
        return pltpu.make_async_copy(getattr(r, name), getattr(r, "keep_" + name), r.save_sem.at[n])

    saves = [save(name, n) for n, name in enumerate(KEPT)]
    for it in saves[:8]:
        it.start()
    loads.wait(*LATER_LOADS)

    def leave(s, carry):
        p = scatter.pair(s)
        for blk in range(4):
            pl.when(p == blk)(partial(attend, r, blk))
        scatter.step(s)
        scatter.put(s, branch_rows(r, rows_at(p * PAIR, PAIR)))
        return carry

    lax.fori_loop(0, 4, leave, 0)
    for it in saves[8:]:
        it.start()
    scatter.step_now(4)
    r.new_stream[...] = r.stream[...].astype(f32) + scatter.finish()
    gather.finish()
    for it in saves:
        it.wait()


def first_layer(stream, norm_params, weights, tables):
    lay = Layout()
    lay.add_in("stream", IN_VMEM, stream)
    add_layer_inputs(lay, norm_params, 0, weights, tables)
    lay.add_out("new_stream", IN_VMEM, (PIECE, D), f32)
    for name, shape in KEPT.items():
        lay.add_out("keep_" + name, IN_HBM, shape, f32 if name == "lse" else bf16)
    lay.add_scratch("vt", pltpu.VMEM((128, LEN), bf16))
    lay.add_scratch("save_sem", pltpu.SemaphoreType.DMA((len(KEPT),)))
    add_gather(lay, "gx")
    add_scatter(lay, "sf")
    return lay.call(first_body, "first", 0)


def middle_body(r):
    ring = Ring()
    gather = Gather(ring, r.xf, r.gxs, r.gxr)
    gather_d = Gather(ring, r.db, r.gds, r.gdr)
    out = scatter_of(r, ring, "sf")
    back = scatter_of(r, ring, "sb")
    loads = Loads(r, 1, ())
    loads.start(*FIRST_LOADS, *LATER_LOADS)
    own = rows_at(ring.me * PIECE, PIECE)
    r.xf[own] = centred_rows(r.stream[...])[0].astype(bf16)
    ring.greet()
    gather.start()
    r.db[own] = r.grad[...].astype(bf16)
    clear(r)
    loads.wait(*FIRST_LOADS)

    def arrive(s, carry):
        gather.step(s)
        pl.when(s == 2)(gather_d.start)
        forward_rows(r, rows_at(gather.pair(s) * PAIR, PAIR))
        return carry

    lax.fori_loop(0, 4, arrive, 0)
    loads.wait(*LATER_LOADS)
    r.kt[...] = r.k[...].astype(f32).T.astype(bf16)

    def leave(s, carry):
        p = out.pair(s)
        for blk in range(4):
            pl.when(p == blk)(partial(attend, r, blk))
        gather_d.step(s)
        out.put(s, branch_rows(r, rows_at(p * PAIR, PAIR)))
        return carry

    lax.fori_loop(0, 4, leave, 0)

    def turn(s, carry):
        out.step(s + 1)
        backward_rows(r, rows_at(s * PAIR, PAIR))
        return carry

    lax.fori_loop(0, 4, turn, 0)
    for blk in range(4):
        attend_back(r, blk)
        if blk == 0:
            r.new_stream[...] = r.stream[...] + out.finish()
    leave_backward(r, back)
    adapter_grads(r, r.own_g, r.all_g, r.norm_o)
    r.new_grad[...] = r.grad[...] + norm_back(r.stream[...], back.finish())
    gather.finish()
    gather_d.finish()


def leave_backward(r, back):
    def leave(s, carry):
        rows = rows_at(back.pair(s) * PAIR, PAIR)
        back.put(s, stream_grad_rows(r, rows))
        down_grad_rows(r, rows)
        back.step(s + 1)
        return carry

    lax.fori_loop(0, 4, leave, 0)


def add_backward(lay):
    lay.add_out("new_grad", IN_VMEM, (PIECE, D), f32)
    lay.add_out("own_g", IN_VMEM, (12, 128, 128), bf16)
    lay.add_out("all_g", IN_VMEM, (8, 512, 128), bf16)
    lay.add_out("norm_o", IN_VMEM, (8, 8, 128), f32)
    lay.add_vmem(BACK, bf16)
    lay.add_vmem(BACK_WIDE, f32)
    add_gather(lay, "gd")
    add_scatter(lay, "sb")


def middle_layer(stream, grad, norm_params, weights, tables):
    lay = Layout()
    lay.add_in("stream", IN_VMEM, stream)
    lay.add_in("grad", IN_VMEM, grad)
    add_layer_inputs(lay, norm_params, 1, weights, tables)
    lay.add_out("new_stream", IN_VMEM, (PIECE, D), f32)
    lay.add_scratch("vt", pltpu.VMEM((128, LEN), bf16))
    add_gather(lay, "gx")
    add_scatter(lay, "sf")
    add_backward(lay)
    return lay.call(middle_body, "middle", 1)


def last_body(r):
    ring = Ring()
    gather_d = Gather(ring, r.db, r.gds, r.gdr)
    back = scatter_of(r, ring, "sb")
    loads = Loads(r, 0, KEPT)
    early = ("oush", "out_w", "od", "down", "sd", "gp", "eu", "up", "ed", "xf")
    then = ("k", "q", "v", "lse", "cos", "sin", "wq", "qu")
    late = ("ias", "le", "act", "att", "lq")
    loads.start(*early, *then, *late)
    r.db[rows_at(ring.me * PIECE, PIECE)] = r.grad[...].astype(bf16)
    ring.greet()
    gather_d.start()
    clear(r)
    loads.wait(*early)

    def arrive(s, carry):
        gather_d.step(s)
        backward_rows(r, rows_at(gather_d.pair(s) * PAIR, PAIR))
        return carry

    lax.fori_loop(0, 4, arrive, 0)
    loads.wait(*then)
    r.kt[...] = r.k[...].astype(f32).T.astype(bf16)
    for blk in range(4):
        attend_back(r, blk)
    loads.wait(*late)
    leave_backward(r, back)
    adapter_grads(r, r.own_g, r.all_g, r.norm_o)
    r.new_grad[...] = r.grad[...] + norm_back(r.stream[...].astype(f32), back.finish())
    gather_d.finish()


def last_layer(stream, grad, norm_params, weights, tables, kept):
    lay = Layout()
    lay.add_in("stream", IN_VMEM, stream)
    lay.add_in("grad", IN_VMEM, grad)
    add_layer_inputs(lay, norm_params, 0, weights, tables, kept)
    add_backward(lay)
    return lay.call(last_body, "last", 2)


def block_homes():
    member, place, at = [], [], np.zeros((LAYERS, 8, 16), np.int32)
    for layer in range(LAYERS):
        for k, count in enumerate(KIND_COUNT):
            for i in range(count):
                each = count // 8
                j = {0: 12, 1: i % 3, 2: 3, 3: 13, 4: 14, 5: 4 + i % 4, 6: 8 + i % 4, 7: 15}[k]
                y, x = j // 4, j % 4
                at[layer, i // each, j] = len(member)
                member.append(i // each)
                place.append(x * 4 + y if layer == 0 else 16 + y * 4 + x)
    return np.array(member, np.int32), np.array(place, np.int32), at


KIND_COUNT = (8, 24, 8, 8, 8, 32, 32, 8)
HOME_MEMBER, HOME_PLACE, BLOCK_AT = block_homes()
PLACE_KIND = np.array([1, 1, 1, 2, 5, 5, 5, 5, 6, 6, 6, 6, 0, 3, 4, 7], np.int32)
PLACE_EACH = np.array([3, 3, 3, 1, 4, 4, 4, 4, 4, 4, 4, 4, 1, 1, 1, 1], np.int32)
PLACE_REST = np.array([0, 1, 2, 0, 0, 1, 2, 3, 0, 1, 2, 3, 0, 0, 0, 0], np.int32)
SLOTS = 3
PARTS = (96, 80, 80)


def route_kernel(ids, owner, at, gathered, out, chosen):
    dp, mp, m = ids[0], ids[1], pl.program_id(0)
    for layer in range(LAYERS):
        slot = owner[at[(layer * 8 + m) * 16 + dp]]
        here = jnp.where(slot // SLOTS % 8 == mp, 1.0, 0.0).astype(bf16)
        for side in range(2):
            out[2 * layer + side] = gathered[slot // (8 * SLOTS), side * SLOTS + slot % SLOTS] * here

    @pl.when(m == 0)
    def _():
        for t in range(8 * SLOTS):
            chosen[0, t] = -1
        for layer in range(LAYERS):
            for j in range(16):
                y, x = j // 4, j % 4
                slot = owner[at[(layer * 8 + mp) * 16 + j]]

                @pl.when(slot // (8 * SLOTS) == dp)
                def _(slot=slot, place=x * 4 + y if layer == 0 else 16 + y * 4 + x):
                    chosen[0, slot % (8 * SLOTS)] = place


def route(ids, owner_slot, gathered):
    return pl.pallas_call(
        route_kernel,
        grid_spec=pltpu.PrefetchScalarGridSpec(
            num_scalar_prefetch=3,
            grid=(8,),
            in_specs=[pl.BlockSpec(memory_space=pltpu.VMEM)],
            out_specs=[
                pl.BlockSpec((None, 2 * LAYERS, RANK, RANK), lambda m, i, o, a: (m, 0, 0, 0)),
                pl.BlockSpec(memory_space=pltpu.SMEM),
            ],
        ),
        out_shape=[
            jax.ShapeDtypeStruct((8, 2 * LAYERS, RANK, RANK), bf16),
            jax.ShapeDtypeStruct((1, 8 * SLOTS), jnp.int32),
        ],
        compiler_params=pltpu.CompilerParams(vmem_limit_bytes=VMEM_LIMIT),
        name="route",
    )(ids, owner_slot, jnp.asarray(BLOCK_AT.reshape(-1)), gathered)


class Axis:
    def __init__(self, name):
        dp, mp = lax.axis_index("dp"), lax.axis_index("mp")
        y, x, z, c = dp // 4, dp % 4, mp // 2, mp % 2
        self.pos = {"x": x, "y": y, "z": z}[name]
        self.plus, self.minus, self.opp = (self.pos + 1) % 4, (self.pos + 3) % 4, (self.pos + 2) % 4

        def device(p):
            if name == "x":
                return {"dp": y * 4 + p}
            if name == "y":
                return {"dp": p * 4 + x}
            return {"mp": p * 2 + c}

        self.up, self.down = device(self.plus), device(self.minus)


def copy_to(src, dst, ssem, rsem, device):
    return pltpu.make_async_remote_copy(
        src_ref=src, dst_ref=dst, send_sem=ssem, recv_sem=rsem, device_id=device, device_id_type=MESH
    )


class AxisGather:
    def __init__(self, axis, buf, rows, split, ssem, rsem):
        self.axis, self.buf, self.ssem, self.rsem = axis, buf, ssem, rsem
        self.halves = (pl.ds(0, split), pl.ds(split, rows - split))

    def cp(self, k, half, sem, device):
        ref = self.buf(k).at[self.halves[half]]
        return copy_to(ref, ref, self.ssem.at[sem], self.rsem.at[sem], device)

    def start(self):
        a = self.axis
        self.cp(a.pos, 0, 0, a.up).start()
        self.cp(a.pos, 1, 1, a.down).start()
        self.cp(a.pos, 1, 2, a.up).start()
        self.cp(a.pos, 0, 3, a.down).start()

    def forward(self, on=None):
        a = self.axis
        self.cp(a.minus, 0, 0, a.up).wait_recv()
        self.cp(a.minus, 0, 4, a.up).start()
        self.cp(a.plus, 1, 1, a.down).wait_recv()
        self.cp(a.plus, 1, 5, a.down).start()
        if on is not None:
            on(0, self.buf(a.minus).at[self.halves[0]])
            on(1, self.buf(a.plus).at[self.halves[1]])

    def wait(self, on=None):
        a = self.axis
        for n, (k, half, sem) in enumerate(((a.minus, 1, 2), (a.plus, 0, 3), (a.opp, 0, 4), (a.opp, 1, 5))):
            self.cp(k, half, sem, a.up).wait_recv()
            if on is not None:
                on(2 + n, self.buf(k).at[self.halves[half]])

    def finish(self):
        a = self.axis
        for half, sem in ((0, 0), (1, 1), (1, 2), (0, 3), (0, 4), (1, 5)):
            self.cp(a.pos, half, sem, a.up).wait_send()


class AxisScatter:
    def __init__(self, axis, terms, rows, split, tr, fin, ssem, rsem):
        self.axis, self.terms, self.tr, self.fin, self.ssem, self.rsem = axis, terms, tr, fin, ssem, rsem
        self.halves = (pl.ds(0, split), pl.ds(split, rows - split))
        self.sizes = (split, rows - split)

    def copies(self):
        a, t, (h0, h1) = self.axis, self.terms, self.halves
        n0, n1 = self.sizes
        return (
            (t(a.opp).at[h0], self.tr.at[0, pl.ds(0, n0)], 0, a.up),
            (t(a.opp).at[h1], self.tr.at[1, pl.ds(0, n1)], 1, a.down),
            (t(a.plus).at[h1], self.fin.at[0, h1], 2, a.up),
            (t(a.minus).at[h0], self.fin.at[1, h0], 3, a.down),
            (t(a.plus).at[h0], self.fin.at[0, h0], 4, a.up),
            (t(a.minus).at[h1], self.fin.at[1, h1], 5, a.down),
        )

    def cp(self, n):
        src, dst, sem, device = self.copies()[n]
        return copy_to(src, dst, self.ssem.at[sem], self.rsem.at[sem], device)

    def start(self):
        for n in range(4):
            self.cp(n).start()

    def middle(self):
        for n in range(2):
            self.cp(n).wait_recv()
            k = (self.axis.plus, self.axis.minus)[n]
            part = self.terms(k).at[self.halves[n]]
            part[...] = (part[...].astype(f32) + self.tr[n, 0 : self.sizes[n]].astype(f32)).astype(bf16)
            self.cp(4 + n).start()

    def total(self):
        for n in range(2, 6):
            self.cp(n).wait_recv()
        return self.terms(self.axis.pos)[...].astype(f32) + self.fin[0].astype(f32) + self.fin[1].astype(f32)

    def finish(self):
        for n in range(6):
            self.cp(n).wait_send()


class MemberScatter:
    def __init__(self, ring, axis, terms, rows, split, prt, mid, tr, fin, psem, qsem, ssem, rsem):
        self.ring, self.terms, self.prt, self.mid, self.psem, self.qsem = ring, terms, prt, mid, psem, qsem
        self.inner = AxisScatter(axis, lambda k: mid.at[k], rows, split, tr, fin, ssem, rsem)
        self.order = (axis.opp, axis.plus, axis.minus, axis.pos)

    def to_partner(self, n):
        r, k = self.ring, self.order[n]
        return copy_to(
            self.terms.at[2 * k + 1 - r.c], self.prt.at[n], self.psem.at[n], self.qsem.at[n], {"mp": r.O}
        )

    def start(self):
        for n in range(4):
            self.to_partner(n).start()

    def add(self, n):
        self.to_partner(n).wait_recv()
        k = self.order[n]
        own = self.terms[2 * k + self.ring.c].astype(f32)
        self.mid[k] = (own + self.prt[n].astype(f32)).astype(bf16)

    def run(self):
        a = self.inner
        self.add(0)
        a.cp(0).start()
        a.cp(1).start()
        self.add(1)
        a.cp(2).start()
        self.add(2)
        a.cp(3).start()
        a.middle()
        self.add(3)
        return a.total()

    def finish(self):
        for n in range(4):
            self.to_partner(n).wait_send()
        self.inner.finish()


LIST_ROWS, LIST_SPLIT = 16 + 8 * 128, 16 + 4 * 128
ROWS_A, ROWS_B = 16 + 4 * 128, 4 * 128
SLOT_ROWS = SLOTS * 128


def update_kernel(
    chosen, own0, own1, all0, all1, norm0, norm1, weights, roots, left_old, right_old,
    grad_o, left_o, right_o, norm_o, full0_o, full1_o, full2_o,
    terms, prt, mid, tr, fin, a1, a1t, a1f, b1, b1t, b1f, a2, a2t, a2f, b2, b2t, b2f, lists,
    terms2, prt2, mid2, tr2, fin2, full0, full1, full2, norm_full,
    mp_p, mp_q, mp_s, mp_r, ax_s, ax_r, mp2_p, mp2_q, mp2_s, mp2_r, ag_s, ag_r, pair_s, pair_r, nm_s, nm_r, osem,
):
    ring = Ring()
    ax, ay, az = Axis("x"), Axis("y"), Axis("z")
    for i in range(8):
        terms[i, 0:16] = jnp.concatenate([norm0[i], norm1[i]], axis=0).astype(bf16)
        terms[i, 16:LIST_SPLIT] = all0[i]
        terms[i, LIST_SPLIT:LIST_ROWS] = all1[i]
    barrier = pltpu.get_barrier_semaphore()
    for device in (ax.up, ax.down, ay.up, ay.down, {"mp": ring.R}, {"mp": ring.L}, {"mp": ring.O}):
        pl.semaphore_signal(barrier, inc=1, device_id=device, device_id_type=MESH)
    pl.semaphore_wait(barrier, 7)

    over_mp = MemberScatter(ring, az, terms, LIST_ROWS, LIST_SPLIT, prt, mid, tr, fin, mp_p, mp_q, mp_s, mp_r)
    over_mp.start()
    for j in range(12):
        y, x = j // 4, j % 4
        a1[x, 16 + y * 128 : 144 + y * 128] = own0[j]
        b1[y, x * 128 : x * 128 + 128] = own1[j]
    summed = over_mp.run()
    for j in range(12, 16):
        y, x = j // 4, j % 4
        at = 16 + (j - 12) * 128
        a1[x, 16 + y * 128 : 144 + y * 128] = summed[at : at + 128].astype(bf16)
        b1[y, x * 128 : x * 128 + 128] = summed[at + 512 : at + 640].astype(bf16)
    for x in range(4):
        a1[x, 0:16] = summed[0:16].astype(bf16)
    sa1 = AxisScatter(ax, lambda k: a1.at[k], ROWS_A, 272, a1t, a1f, ax_s.at[0], ax_r.at[0])
    sb1 = AxisScatter(ay, lambda k: b1.at[k], ROWS_B, 256, b1t, b1f, ax_s.at[1], ax_r.at[1])
    sa1.start()
    sb1.start()
    sa1.middle()
    sb1.middle()
    got = sa1.total()
    for y in range(4):
        a2[y, 0:16] = got[0:16].astype(bf16)
        a2[y, 16:144] = got[16 + y * 128 : 144 + y * 128].astype(bf16)
    sa2 = AxisScatter(ay, lambda k: a2.at[k], 144, 80, a2t, a2f, ax_s.at[2], ax_r.at[2])
    sa2.start()
    got = sb1.total()
    for x in range(4):
        b2[x] = got[x * 128 : x * 128 + 128].astype(bf16)
    sb2 = AxisScatter(ax, lambda k: b2.at[k], 128, 64, b2t, b2f, ax_s.at[3], ax_r.at[3])
    sb2.start()
    sa2.middle()
    sb2.middle()

    x, y, z, c = ax.pos, ay.pos, az.pos, ring.c
    got = sa2.total()
    norm_full[pl.ds(pl.multiple_of(ring.me * 16, 16), 16)] = got[0:16]
    blocks_here = (got[16:144].astype(bf16), sb2.total().astype(bf16))
    lists[x * 4 + y] = blocks_here[0]
    lists[16 + y * 4 + x] = blocks_here[1]
    stepped = []
    for layer in range(LAYERS):
        way = nn(roots[2 * layer], blocks_here[layer]).astype(bf16)
        way = nn(way, roots[2 * layer + 1])
        w = weights[layer]
        size = jnp.sqrt(jnp.mean(w * w) + STEP_EPS) * lax.rsqrt(jnp.mean(way * way) + STEP_EPS)
        stepped.append((w - ADAPT_RATE * size * way).astype(bf16))
    full0[c, y, x, z] = stepped[0][0:96]
    full1[c, z, y, x] = jnp.concatenate([stepped[0][96:128], stepped[1][0:48]], axis=0)
    full2[c, x, z, y] = stepped[1][48:128]

    places = ((az, ax, ay), (ax, ay, az), (ay, az, ax))
    fulls = (full0, full1, full2)
    stages = []
    for j, rows in enumerate(PARTS):
        first, second, third = places[j]
        t, u, full = third.pos, second.pos, fulls[j]
        seconds = full.reshape(2, 4, 4, 4 * rows, 128)
        thirds = full.reshape(2, 4, 16 * rows, 128)
        half = rows // 32 * 16
        stages.append(
            (
                AxisGather(first, lambda k, f=full, t=t, u=u: f.at[c, t, u, k], rows, half, ag_s.at[0, j], ag_r.at[0, j]),
                AxisGather(second, lambda k, f=seconds, t=t: f.at[c, t, k], 4 * rows, 2 * rows, ag_s.at[1, j], ag_r.at[1, j]),
                AxisGather(third, lambda k, f=thirds: f.at[c, k], 16 * rows, 8 * rows, ag_s.at[2, j], ag_r.at[2, j]),
            )
        )
    partner = {"mp": ring.O}

    def to_partner(j, n, ref):
        copy_to(ref, ref, pair_s.at[j, n], pair_r.at[j, n], partner).start()

    def each(stage, what, *on):
        for j in range(3):
            getattr(stages[j][stage], what)(*[f(j) for f in on])

    wide = lists.reshape(8, 4 * 128, 128)
    ga1 = AxisGather(ay, lambda k: lists.at[x * 4 + k], 128, 64, ax_s.at[4], ax_r.at[4])
    gb1 = AxisGather(ax, lambda k: lists.at[16 + y * 4 + k], 128, 64, ax_s.at[5], ax_r.at[5])
    ga2 = AxisGather(ax, lambda k: wide.at[k], 512, 256, ax_s.at[6], ax_r.at[6])
    gb2 = AxisGather(ay, lambda k: wide.at[4 + k], 512, 256, ax_s.at[7], ax_r.at[7])
    norms = Gather(ring, norm_full, nm_s, nm_r, 16)
    to_slots = MemberScatter(
        ring, az, terms2, SLOT_ROWS, SLOT_ROWS // 2, prt2, mid2, tr2, fin2, mp2_p, mp2_q, mp2_s, mp2_r
    )

    each(0, "start")
    ga1.start()
    gb1.start()
    norms.start()
    each(0, "forward")
    ga1.forward()
    gb1.forward()
    each(0, "wait")
    each(1, "start")
    ga1.wait()
    gb1.wait()
    ga2.start()
    gb2.start()
    each(1, "forward")
    ga2.forward()
    gb2.forward()
    each(1, "wait")
    each(2, "start")
    for j in range(3):
        to_partner(j, 6, stages[j][2].buf(places[j][2].pos))
    ga2.wait()
    gb2.wait()
    for t in range(8 * SLOTS):
        at = chosen[0, t]
        here = jnp.where(at >= 0, 1.0, 0.0).astype(bf16)
        terms2[t // SLOTS, (t % SLOTS) * 128 : (t % SLOTS) * 128 + 128] = lists[jnp.maximum(at, 0)] * here
    to_slots.start()
    each(2, "forward", lambda j: partial(to_partner, j))
    own = to_slots.run()
    for j in range(SLOTS):
        g = own[j * 128 : j * 128 + 128]
        gl = g.astype(bf16)
        grad_o[j] = g
        scale = (1 - STAT_DECAY) / (jnp.mean(g * g) + STEP_EPS)
        left_o[j] = STAT_DECAY * left_old[j] + nt(gl, gl) * scale
        right_o[j] = STAT_DECAY * right_old[j] + tn(gl, gl) * scale
    each(2, "wait", lambda j: partial(to_partner, j))
    outs = (full0_o, full1_o, full2_o)
    saves = [pltpu.make_async_copy(fulls[j].at[c], outs[j].at[c], osem.at[0, j]) for j in range(3)]
    for save in saves:
        save.start()
    for s in range(4):
        norms.step_now(s)
    norm_o[...] = norm_full[...]
    for j, rows in enumerate(PARTS):
        theirs = fulls[j].reshape(2, 4, 16 * rows, 128).at[1 - c, 0]
        for n in range(7):
            part = theirs if n == 6 else theirs.at[pl.ds(0, 8 * rows)]
            copy_to(part, part, pair_s.at[j, n], pair_r.at[j, n], partner).wait_recv()
    more = [pltpu.make_async_copy(fulls[j].at[1 - c], outs[j].at[1 - c], osem.at[1, j]) for j in range(3)]
    for save in more:
        save.start()
    for j, rows in enumerate(PARTS):
        mine = fulls[j].reshape(2, 4, 16 * rows, 128).at[c, 0]
        for n in range(7):
            part = mine if n == 6 else mine.at[pl.ds(0, 8 * rows)]
            copy_to(part, part, pair_s.at[j, n], pair_r.at[j, n], partner).wait_send()
    for stage in range(3):
        each(stage, "finish")
    for it in (over_mp, to_slots, sa1, sb1, sa2, sb2, ga1, gb1, ga2, gb2, norms):
        it.finish()
    for save in saves + more:
        save.wait()


def update(chosen, own, every, norms, weights, roots, left, right):
    one = jax.ShapeDtypeStruct((SLOTS, RANK, RANK), f32)
    dma = pltpu.SemaphoreType.DMA
    full_shapes = [(2, 4, 4, 4, rows, 128) for rows in PARTS]

    def scatter_scratch(rows, split):
        return [pltpu.VMEM((4, rows, 128), bf16), pltpu.VMEM((2, split, 128), bf16), pltpu.VMEM((2, rows, 128), bf16)]

    def member_scratch(rows, split):
        return [pltpu.VMEM((8, rows, 128), bf16), pltpu.VMEM((4, rows, 128), bf16)] + scatter_scratch(rows, split)

    return pl.pallas_call(
        update_kernel,
        in_specs=[pl.BlockSpec(memory_space=pltpu.SMEM)] + [IN_VMEM] * 10,
        out_specs=[IN_VMEM] * 4 + [pl.BlockSpec(memory_space=pl.ANY)] * 3,
        out_shape=[one, one, one, jax.ShapeDtypeStruct((128, 128), f32)]
        + [jax.ShapeDtypeStruct(s, bf16) for s in full_shapes],
        scratch_shapes=member_scratch(LIST_ROWS, LIST_SPLIT)
        + scatter_scratch(ROWS_A, 272)
        + scatter_scratch(ROWS_B, 256)
        + scatter_scratch(144, 80)
        + scatter_scratch(128, 64)
        + [pltpu.VMEM((32, 128, 128), bf16)]
        + member_scratch(SLOT_ROWS, SLOT_ROWS // 2)
        + [pltpu.VMEM(s, bf16) for s in full_shapes]
        + [pltpu.VMEM((128, 128), f32)]
        + [dma((4,)), dma((4,)), dma((6,)), dma((6,)), dma((8, 6)), dma((8, 6))]
        + [dma((4,)), dma((4,)), dma((6,)), dma((6,)), dma((3, 3, 6)), dma((3, 3, 6))]
        + [dma((3, 7)), dma((3, 7)), dma((13,)), dma((13,)), dma((2, 3))],
        compiler_params=pltpu.CompilerParams(
            collective_id=3, has_side_effects=True, vmem_limit_bytes=VMEM_LIMIT
        ),
        name="update",
    )(chosen, own[0], own[1], every[0], every[1], norms[0], norms[1], weights, roots, left, right)


def finish_kernel(full0, full1, full2, sums, params, first, second, *refs):
    given, refs = refs[:5], refs[5:]
    outs, (moment_o, square_o, expand_o, new_o), passed = refs[:8], refs[8:12], refs[12:]
    m, layer = pl.program_id(0), pl.program_id(1)

    @pl.when((m == 0) & (layer == 0))
    def _():
        for src, dst in zip(given, passed):
            dst[...] = src[...]
        for l in range(LAYERS):
            g = jnp.concatenate([sums[i * 16 + l * 8 : i * 16 + l * 8 + 8, :] for i in range(8)], axis=1)[0:4]
            moment = MOMENT_DECAY * first[l] + (1 - MOMENT_DECAY) * g
            square = SQUARE_DECAY * second[l] + (1 - SQUARE_DECAY) * g * g
            moment_o[l] = moment
            square_o[l] = square[0:2]
            expand_o[l] = square[2:4]
            scaled = jnp.sqrt(square / (1 - SQUARE_DECAY**ADAM_STEP)) + ADAM_EPS
            new_o[l] = params[l] - NORM_RATE * (moment / (1 - MOMENT_DECAY**ADAM_STEP)) / scaled

    def put(l):
        for i in range(2):
            for j in range(16):
                y, x = j // 4, j % 4
                if l == 0:
                    block = jnp.concatenate([full0[i, y, x], full1[i, y, x, 0:32]], axis=0)
                else:
                    block = jnp.concatenate([full1[i, y, x, 32:80], full2[i, x, y]], axis=0)
                k = int(PLACE_KIND[j])
                n = (i * int(PLACE_EACH[j]) + int(PLACE_REST[j])) * 128
                if k % 2 == 1:
                    outs[k][:, n : n + 128] = block.astype(f32)
                else:
                    outs[k][n : n + 128, :] = block.astype(f32)

    for l in range(LAYERS):
        pl.when(layer == l)(partial(put, l))


def finish(fulls, sums, norm_params, norm_first, norm_second, given):
    def spec(k):
        each = KIND_COUNT[k] // 4
        if k % 2 == 1:
            return pl.BlockSpec((None, RANK, each * RANK), lambda m, l: (l, 0, m))
        return pl.BlockSpec((None, each * RANK, RANK), lambda m, l: (l, m, 0))

    def whole(shape):
        return pl.BlockSpec(shape, lambda m, l: (0,) * len(shape))

    shapes = [(LAYERS, RANK, c * RANK) if k % 2 == 1 else (LAYERS, c * RANK, RANK) for k, c in enumerate(KIND_COUNT)]
    norm_shapes = [(LAYERS, 4, D), (LAYERS, 2, D), (LAYERS, 2, D), (LAYERS, 4, D)]
    given_shapes = [g.shape for g in given]
    return pl.pallas_call(
        finish_kernel,
        grid=(4, LAYERS),
        in_specs=[
            pl.BlockSpec((2, 4, 4, None, PARTS[0], 128), lambda m, l: (0, 0, 0, m, 0, 0)),
            pl.BlockSpec((2, None, 4, 4, PARTS[1], 128), lambda m, l: (0, m, 0, 0, 0, 0)),
            pl.BlockSpec((2, 4, None, 4, PARTS[2], 128), lambda m, l: (0, 0, m, 0, 0, 0)),
            whole((128, 128)),
        ]
        + [whole((LAYERS, 4, D))] * 3
        + [whole(g) for g in given_shapes],
        out_specs=[spec(k) for k in range(8)] + [whole(n) for n in norm_shapes] + [whole(g) for g in given_shapes],
        out_shape=[jax.ShapeDtypeStruct(n, f32) for n in shapes + norm_shapes + given_shapes],
        compiler_params=pltpu.CompilerParams(vmem_limit_bytes=VMEM_LIMIT),
        name="finish",
    )(*fulls, sums, norm_params, norm_first, norm_second, *given)


def body(
    hidden_in, cotangent, segments, qkv_weight, out_weight, up_weight, down_weight,
    query_down, query_up, output_down, output_up, expand_down, expand_up, shrink_down, shrink_up,
    norm_params, norm_first, norm_second, owner_slot, left_stats, right_stats, left_roots, right_roots,
):
    adapters = (query_down, query_up, output_down, output_up, expand_down, expand_up, shrink_down, shrink_up)
    ids = jnp.stack([lax.axis_index("dp"), lax.axis_index("mp")]).astype(jnp.int32)
    plan = jnp.concatenate([ids, jnp.asarray(np.concatenate([PLACE_KIND, PLACE_EACH, PLACE_REST]))])
    roots = lax.all_gather(jnp.concatenate([left_roots, right_roots]).astype(bf16), "dp", axis=0)
    prepared = prepare(plan, segments, qkv_weight, adapters)
    weights = tuple(prepared[:7]) + (up_weight, down_weight, out_weight)
    home_weights, tables = prepared[7], prepared[8:]
    made = first_layer(hidden_in, norm_params, weights, tables)
    stream, kept = made[0], made[1:]
    own, every, norms = [None] * LAYERS, [None] * LAYERS, [None] * LAYERS
    hidden_out, grad, own[1], every[1], norms[1] = middle_layer(stream, cotangent, norm_params, weights, tables)
    roots, grad = lax.optimization_barrier((roots, grad))
    routed, chosen = route(ids, owner_slot, roots)
    roots = lax.psum_scatter(routed, "mp", scatter_dimension=0, tiled=False)
    hidden_grad, own[0], every[0], norms[0] = last_layer(hidden_in, grad, norm_params, weights, tables, kept)
    made = update(chosen, own, every, norms, home_weights, roots, left_stats, right_stats)
    given = (hidden_out, hidden_grad) + tuple(made[:3])
    done = finish(made[4:], made[3], norm_params, norm_first, norm_second, given)
    return tuple(done[12:]) + tuple(done[:12])


def solution(mesh):
    both = P(("dp", "mp"))
    cols, rows, copied = P(None, None, "mp"), P(None, "mp", None), P()
    in_specs = (both, both, P("dp"), cols, rows, cols, rows) + (copied,) * 12 + (both,) * 4
    out_specs = (both,) * 5 + (copied,) * 12
    return jax.shard_map(body, mesh=mesh, in_specs=in_specs, out_specs=out_specs, check_vma=False)
```
